768 devices in a mesh: dp: 64 (over y, z_hi, core), expert: 12 (over z_lo, x).
Axes of the slice: x: 4, y: 8, z: 12 (z_hi: 4, z_lo: 3; z = z_hi * 3 + z_lo), core: 2. Of those that a mesh axis runs over, the one named last changes fastest.
Arguments:
- out_grad: bfloat16 [98304, 2560], P(('dp', 'expert')), may hold values from -1.5 to 1.5
- probs: bfloat16 [98304, 3], P(('dp', 'expert')), may hold values from 0.099609375 to 1
- picks: int32 [98304, 3], P(('dp', 'expert')), may hold values from 0 to 3, as said below
- saved_pre: bfloat16 [294912, 1344], P(('dp', 'expert')), may hold values from -6 to 6
- down_weight: bfloat16 [12, 2560, 672], P('expert'), may hold values from -0.125 to 0.125
Outputs:
- pre_grad: bfloat16 [294912, 1344], P(('dp', 'expert'))
- down_grad: float32 [12, 2560, 672], P('expert', 'dp')
- prob_grad: float32 [98304, 3], P(('dp', 'expert'))
The draws below stay inside these ranges and needn't reach their ends.
Inputs may be any that keep to these rules, and one draw needn't show every extreme that they name: `picks`: in each block of 128 tokens and each group, every value is picked by exactly 32 tokens.
All inputs are finite; a program needn't handle non-finite values.
Results may differ from the reference program's by a relative error of at most 0.0031.
Values may be sent and summed in bfloat16 or wider, within the bound.
No kernel may reach another device: no remote copies, remote signals or barrier semaphores. Data moves between devices by JAX's collectives and lax.ppermute only.
A program may use at most 128 MiB of HBM per device.

```python
import jax
import jax.numpy as jnp
from jax import lax

D = 2560
FW = 672
GSIZE = 4
TOK = 128
EXPERTS = 12
NGROUPS = 3
SLOTS = 384
TOKENS = 98304
N_DP = 64
N_EXPERT = 12


def draw_picks(key, part):
    key = jax.random.fold_in(key, 11)
    count = TOKENS // TOK * NGROUPS
    keys = jax.random.split(key, count)
    ranked = jax.vmap(lambda single: jax.random.permutation(single, TOK))(keys)
    values = (ranked % GSIZE).astype(jnp.int32)
    values = values.reshape(TOKENS // TOK, NGROUPS, TOK)
    return jnp.transpose(values, (0, 2, 1)).reshape(TOKENS, NGROUPS)


def level_of(stream_key, dims, pieces, least, largest):
    def one(position, blocks):
        steps = jax.random.uniform(jax.random.fold_in(jax.random.fold_in(stream_key, 6), position), (blocks,), jnp.float32, least / len(pieces), largest / len(pieces))
        return jnp.repeat(jnp.exp(steps), dims[position] // blocks).reshape((-1,) + (1,) * (len(dims) - position - 1))

    loudness = one(*pieces[0])
    for cut in pieces[1:]:
        loudness = loudness * one(*cut)
    return loudness


def gaussian(rng, extent, spread, limit, cuts=(), kind=jnp.bfloat16):
    gain = level_of(rng, extent, cuts, -0.22, 0.18) if cuts else 1.0
    result = jax.random.normal(rng, extent, jnp.float32) * spread * gain
    return jnp.minimum(jnp.maximum(result, -limit), limit).astype(kind)


def setup_inputs(seed: int = 0) -> dict:
    arg_keys = jax.random.split(jax.random.key(seed), 6)
    return {
        "out_grad": gaussian(arg_keys[0], (TOKENS, D), 0.25, 1.5, ((0, 768),)),
        "probs": jnp.clip(0.099609375 + 0.9003906 * jax.random.uniform(arg_keys[1], (TOKENS, NGROUPS), jnp.float32) ** level_of(arg_keys[1], (TOKENS, NGROUPS), ((0, 768),), -0.2, 0.2), 0.099609375, 1.0).astype(jnp.bfloat16),
        "picks": draw_picks(jax.random.fold_in(arg_keys[5], 71), 0),
        "saved_pre": gaussian(arg_keys[3], (N_DP * EXPERTS * SLOTS, 2 * FW), 1.0, 6.0, ((0, 768),)),
        "down_weight": gaussian(arg_keys[4], (EXPERTS, D, FW), D ** -0.5, 0.125, ((0, 12),)),
    }


def reference(out_grad, probs, picks, saved_pre, down_weight):
    blocks = out_grad.reshape(N_DP, N_EXPERT, TOK, D)
    prob_blocks = probs.reshape(N_DP, N_EXPERT, TOK, NGROUPS)
    pick_blocks = picks.reshape(N_DP, N_EXPERT, TOK, NGROUPS)
    ranking = jnp.argsort(pick_blocks, axis=2, stable=True).astype(jnp.int32)
    ranking = jnp.transpose(ranking, (3, 0, 1, 2)).reshape(NGROUPS, N_DP, N_EXPERT, GSIZE, TOK // GSIZE)
    slot_index = jnp.transpose(ranking, (0, 3, 1, 2, 4)).reshape(EXPERTS, N_DP, N_EXPERT, TOK // GSIZE)
    saved_all = jnp.transpose(saved_pre.reshape(N_DP, EXPERTS, SLOTS, 2 * FW), (1, 0, 2, 3))

    def per_expert(inputs):
        expert_id, index_here, saved_here, weight = inputs
        group_id = expert_id // GSIZE
        slot_rows = jnp.take_along_axis(blocks, index_here[..., None], axis=2).reshape(N_DP, SLOTS, D)
        group_probs = jnp.take(prob_blocks, group_id, axis=3)
        slot_prob = jnp.take_along_axis(group_probs, index_here, axis=2).reshape(N_DP, SLOTS).astype(jnp.float32)
        gate_part = saved_here[..., :FW].astype(jnp.float32)
        up_part = saved_here[..., FW:].astype(jnp.float32)
        sigmoid_g = jax.nn.sigmoid(gate_part)
        activated = gate_part * sigmoid_g
        hidden = activated * up_part
        projected = jnp.einsum("rsd,df->rsf", slot_rows.astype(jnp.float32), weight.astype(jnp.float32),
                               precision=lax.Precision.HIGHEST)
        slot_grad = jnp.sum(hidden * projected, axis=-1)
        hidden_grad = slot_prob[..., None] * projected
        gate_grad = hidden_grad * up_part * sigmoid_g * (1.0 + gate_part * (1.0 - sigmoid_g))
        up_grad = hidden_grad * activated
        pre_grad = jnp.concatenate([gate_grad, up_grad], axis=-1).astype(jnp.bfloat16)
        scaled_hidden = (slot_prob[..., None] * hidden).astype(jnp.bfloat16)
        weight_grad = jnp.einsum("rsd,rsf->df", slot_rows.astype(jnp.float32), scaled_hidden.astype(jnp.float32),
                                 precision=lax.Precision.HIGHEST)
        return pre_grad, weight_grad, slot_grad

    expert_ids = jnp.arange(EXPERTS, dtype=jnp.int32)
    pre_all, down_grad, slot_all = lax.map(per_expert, (expert_ids, slot_index, saved_all, down_weight))
    pre_grad = jnp.transpose(pre_all, (1, 0, 2, 3)).reshape(N_DP * EXPERTS * SLOTS, 2 * FW)
    shape_all = (EXPERTS, N_DP, N_EXPERT, TOK // GSIZE)
    replica_ids = jnp.broadcast_to(jnp.arange(N_DP, dtype=jnp.int32)[None, :, None, None], shape_all)
    source_ids = jnp.broadcast_to(jnp.arange(N_EXPERT, dtype=jnp.int32)[None, None, :, None], shape_all)
    group_ids = jnp.broadcast_to((expert_ids // GSIZE)[:, None, None, None], shape_all)
    slot_values = slot_all.reshape(shape_all)
    prob_grad = jnp.zeros((N_DP, N_EXPERT, TOK, NGROUPS), jnp.float32)
    prob_grad = prob_grad.at[replica_ids, source_ids, slot_index, group_ids].set(slot_values)
    return pre_grad, down_grad, prob_grad.reshape(TOKENS, NGROUPS)
```

```python
import functools

import jax
import jax.numpy as jnp
import numpy as np
from jax import lax
from jax.experimental import pallas as pl
from jax.experimental.pallas import tpu as pltpu
from jax.sharding import Mesh, PartitionSpec as P

BF = jnp.bfloat16
F32 = jnp.float32
NY, NZ, NC, NZL, NX = 8, 4, 2, 3, 4
D, FW, TOK, SLOTS, OWN = 2560, 672, 128, 384, 40
HALF = D // 2
WIDE = D + 128
ROWS_T = (((0,), (0,)), ((), ()))
LANES_T = (((1,), (1,)), ((), ()))


def split_matrix():
    m = np.zeros((HALF, HALF), np.float32)
    n = np.arange(HALF)
    h, rest = n // 640, n % 640
    m[80 * (rest // OWN) + OWN * h + rest % OWN, n] = 1.0
    return m


def params(mib=48):
    return pltpu.CompilerParams(vmem_limit_bytes=mib * 1024 * 1024)


def one_hot(mask):
    return jnp.where(mask, 1.0, 0.0).astype(BF)


def pick_kernel(core_ref, picks_ref, probs_ref, og_ref, q_ref, out_ref, pos_ref, x_ref):
    core = core_ref[0]
    for p in range(2):
        y = jnp.dot(og_ref[:, HALF * p : HALF * (p + 1)], q_ref[...], preferred_element_type=F32).astype(BF)
        for h in range(2):
            at = pl.multiple_of((core ^ h) * HALF + 640 * p, 128)
            x_ref[:, pl.ds(at, 640)] = y[:, 640 * h : 640 * (h + 1)]
    row = lax.broadcasted_iota(jnp.int32, (TOK, TOK), 0)
    col = lax.broadcasted_iota(jnp.int32, (TOK, TOK), 1)
    before = one_hot(row < col)
    value = lax.broadcasted_iota(jnp.int32, (16, TOK), 0)
    for g in range(3):
        chosen = picks_ref[g : g + 1, :] == value
        rank = jnp.dot(one_hot(chosen), before, preferred_element_type=F32)
        pos = jnp.sum(jnp.where(chosen, rank + 32.0 * value.astype(F32), 0.0), axis=0, keepdims=True)
        pos = pos.astype(jnp.int32)
        pos_ref[g : g + 1, :] = pos
        sel = row == pos
        out_ref[g * TOK : (g + 1) * TOK, :D] = jnp.dot(
            one_hot(sel), x_ref[...], preferred_element_type=F32
        ).astype(BF)
        pr = jnp.sum(
            jnp.where(sel, probs_ref[g : g + 1, :].astype(F32), 0.0), axis=1, keepdims=True
        )
        out_ref[g * TOK : (g + 1) * TOK, D:] = jnp.broadcast_to(pr, (TOK, 128)).astype(BF)


def order_kernel(core_ref, w_ref, q_ref, out_ref):
    core = core_ref[0]
    for p in range(2):
        y = jnp.dot(w_ref[:, HALF * p : HALF * (p + 1)], q_ref[...], preferred_element_type=F32).astype(BF)
        for h in range(2):
            at = pl.multiple_of((core ^ h) * HALF + 640 * p, 128)
            out_ref[:, pl.ds(at, 640)] = y[:, 640 * h : 640 * (h + 1)]


def hidden_kernel(own_ref, peer_ref, out_ref):
    for k, ref in enumerate((own_ref, peer_ref)):
        gate = ref[:FW, :].astype(F32)
        up = ref[FW:, :].astype(F32)
        hid = gate * jax.nn.sigmoid(gate) * up
        out_ref[k * SLOTS : (k + 1) * SLOTS, :] = hid.T


def grad_kernel(own_ref, prob_ref, peer_ref, hid_ref, out_ref, sh_ref):
    for k in range(2):
        p = (prob_ref[...] if k == 0 else peer_ref[:, HALF:]).astype(F32)
        for a in range(0, FW, 128):
            b = min(a + 128, FW)
            sh_ref[k * SLOTS : (k + 1) * SLOTS, a:b] = (
                p[:, : b - a] * hid_ref[k * SLOTS : (k + 1) * SLOTS, a:b]
            ).astype(BF)
    for a in range(0, HALF, 128):
        acc = lax.dot_general(
            own_ref[:, a : a + 128], sh_ref[:SLOTS, :], ROWS_T, preferred_element_type=F32
        )
        acc += lax.dot_general(
            peer_ref[:, a : a + 128], sh_ref[SLOTS:, :], ROWS_T, preferred_element_type=F32
        )
        out_ref[a : a + 128, :] = acc.astype(BF)


def pre_kernel(w_ref, rows_ref, sp_ref, pg_ref, sg_ref):
    lane = lax.broadcasted_iota(jnp.int32, (16, 128), 1)
    prob = lax.dot_general(
        one_hot(lane == 0), rows_ref[:, D:], LANES_T, preferred_element_type=F32
    )[:1]
    total = jnp.zeros((1, SLOTS), F32)
    step = FW // 3
    for a in range(0, FW, step):
        proj = lax.dot_general(
            w_ref[a : a + step, :], rows_ref[:, :D], LANES_T, preferred_element_type=F32
        )
        gate = sp_ref[a : a + step, :].astype(F32)
        up = sp_ref[FW + a : FW + a + step, :].astype(F32)
        sig = jax.nn.sigmoid(gate)
        act = gate * sig
        total += jnp.sum(act * up * proj, axis=0, keepdims=True)
        hg = prob * proj
        pg_ref[a : a + step, :] = (hg * up * sig * (1.0 + gate * (1.0 - sig))).astype(BF)
        pg_ref[FW + a : FW + a + step, :] = (hg * act).astype(BF)
    sg_ref[...] = total


def back_kernel(pos_ref, ret_ref, out_ref):
    row = lax.broadcasted_iota(jnp.int32, (TOK, TOK), 0)
    for g in range(3):
        sel = jnp.where(row == pos_ref[g : g + 1, :], 1.0, 0.0)
        val = jnp.broadcast_to(ret_ref[g : g + 1, :], (8, TOK))
        out_ref[g : g + 1, :] = jnp.dot(
            val, sel, preferred_element_type=F32, precision=lax.Precision.HIGHEST
        )[:1]


def cost(macs, nbytes):
    return pl.CostEstimate(flops=2 * macs, bytes_accessed=nbytes, transcendentals=0)


SMEM = pl.BlockSpec(memory_space=pltpu.SMEM)
VMEM = pl.BlockSpec(memory_space=pltpu.VMEM)


def on_device(out_grad, probs, picks, saved_pre, down_weight):
    core = lax.axis_index("c")
    core1 = core.astype(jnp.int32).reshape(1)
    swap = [(0, 1), (1, 0)]
    q = jnp.asarray(split_matrix(), BF)
    sp_t = saved_pre.T
    w_t = down_weight[0].T
    send, pos = pl.pallas_call(
        pick_kernel,
        out_shape=(
            jax.ShapeDtypeStruct((SLOTS, WIDE), BF),
            jax.ShapeDtypeStruct((3, TOK), jnp.int32),
        ),
        in_specs=[SMEM, VMEM, VMEM, VMEM, VMEM],
        out_specs=(VMEM, VMEM),
        scratch_shapes=[pltpu.VMEM((TOK, D), BF)],
        compiler_params=params(),
        cost_estimate=cost(500_000_000, 7_000_000),
        name="pick",
    )(core1, picks.T, probs.T, out_grad, q)
    recv = lax.all_to_all(
        send.reshape(12, 32, WIDE), ("zl", "x"), split_axis=0, concat_axis=0, tiled=True
    ).reshape(SLOTS, WIDE)

    sp_peer = lax.ppermute(sp_t, "c", swap)
    hid = pl.pallas_call(
        hidden_kernel,
        out_shape=jax.ShapeDtypeStruct((2 * SLOTS, FW), F32),
        in_specs=[VMEM, VMEM],
        out_specs=VMEM,
        compiler_params=params(),
        cost_estimate=cost(500_000_000, 7_000_000),
        name="hidden",
    )(sp_t, sp_peer)
    w_ord = pl.pallas_call(
        order_kernel,
        out_shape=jax.ShapeDtypeStruct((FW, D), BF),
        in_specs=[SMEM, VMEM, VMEM],
        out_specs=VMEM,
        compiler_params=params(),
        cost_estimate=cost(2_000_000_000, 10_000_000),
        name="order",
    )(core1, w_t, q)

    peer = lax.ppermute(recv[:, HALF:], "c", swap)
    part = pl.pallas_call(
        grad_kernel,
        grid=(1,),
        out_shape=jax.ShapeDtypeStruct((HALF, FW), BF),
        in_specs=[
            pl.BlockSpec((SLOTS, HALF), lambda i: (0, 0)),
            pl.BlockSpec((SLOTS, 128), lambda i: (0, D // 128)),
            pl.BlockSpec((SLOTS, HALF + 128), lambda i: (0, 0)),
            pl.BlockSpec((2 * SLOTS, FW), lambda i: (0, 0)),
        ],
        out_specs=pl.BlockSpec((HALF, FW), lambda i: (0, 0)),
        scratch_shapes=[pltpu.VMEM((2 * SLOTS, FW), BF)],
        compiler_params=params(),
        cost_estimate=cost(700_000_000, 7_000_000),
        name="grad",
    )(recv, recv, peer, hid)
    over_y = lax.all_to_all(
        part.reshape(NY, HALF // NY, FW), "y", split_axis=0, concat_axis=0, tiled=True
    )
    sum_y = jnp.sum(over_y.astype(F32), axis=0).astype(BF)
    over_z = lax.all_to_all(
        sum_y.reshape(NZ, OWN, FW), "z", split_axis=0, concat_axis=0, tiled=True
    )
    down_grad = jnp.sum(over_z.astype(F32), axis=0)

    pg_t, slot_grad = pl.pallas_call(
        pre_kernel,
        out_shape=(
            jax.ShapeDtypeStruct((2 * FW, SLOTS), BF),
            jax.ShapeDtypeStruct((1, SLOTS), F32),
        ),
        in_specs=[VMEM, VMEM, VMEM],
        out_specs=(VMEM, VMEM),
        compiler_params=params(),
        cost_estimate=cost(1_000_000_000, 8_000_000),
        name="pre",
    )(w_ord, recv, sp_t)
    every = lax.all_gather(slot_grad, ("zl", "x"), axis=0, tiled=True)
    here = lax.axis_index("zl") * NX + lax.axis_index("x")
    ret = lax.dynamic_slice(every, (0, here * 32), (12, 32)).reshape(3, TOK)
    prob_t = pl.pallas_call(
        back_kernel,
        out_shape=jax.ShapeDtypeStruct((3, TOK), F32),
        in_specs=[VMEM, VMEM],
        out_specs=VMEM,
        name="back",
    )(pos, ret)
    return (pg_t.T, down_grad[None], prob_t.T)


def solution(mesh):
    cut = Mesh(mesh.devices.reshape(NY, NZ, NC, NZL, NX), ("y", "z", "c", "zl", "x"))
    rows = P(("y", "z", "c", "zl", "x"), None)
    in_specs = (rows, rows, rows, rows, P(("zl", "x"), None, None))
    out_specs = (rows, P(("zl", "x"), ("y", "z", "c"), None), rows)
    return jax.shard_map(
        on_device, mesh=cut, in_specs=in_specs, out_specs=out_specs, check_vma=False
    )
```

```python
import jax
import jax.numpy as jnp
import numpy as np
from jax import lax
from jax.experimental import pallas as pl
from jax.experimental.pallas import tpu as pltpu
from jax.sharding import Mesh, PartitionSpec as P

BF = jnp.bfloat16
F32 = jnp.float32
NK, NP, NZ, NC, NZL, NX = 4, 2, 4, 2, 3, 4
D, FW, TOK, SLOTS, OWN = 2560, 672, 128, 384, 40
BLK = D // NK
PART = BLK // 4
CH = NK * PART
ROWS_T = (((0,), (0,)), ((), ()))
LANES_T = (((1,), (1,)), ((), ()))


def split_matrices():
    m = np.zeros((2, BLK, 2 * PART), np.float32)
    for chunk in range(2):
        n = np.arange(2 * PART)
        h, par, z, i = n // PART, n % PART // 80, n % 80 // OWN, n % OWN
        m[chunk, par * 320 + (2 * chunk + z) * 80 + h * OWN + i, n] = 1.0
    return m.reshape(2 * BLK, 2 * PART)


def one_hot(mask):
    return jnp.where(mask, 1.0, 0.0).astype(BF)


def reorder(ref, q_ref, core, out_ref, base):
    y = [
        jnp.dot(ref[:, BLK * k : BLK * (k + 1)], q_ref[...], preferred_element_type=F32)
        for k in range(NK)
    ]
    for h in range(2):
        at = pl.multiple_of((core ^ h) * CH + base, 128)
        out_ref[:, pl.ds(at, CH)] = jnp.concatenate(
            [v[:, PART * h : PART * (h + 1)] for v in y], axis=1
        ).astype(BF)


def first_pick_kernel(core_ref, picks_ref, probs_ref, og_ref, q_ref, out_ref, pos_ref, x_ref):
    reorder(og_ref, q_ref, core_ref[0], x_ref, 0)
    row = lax.broadcasted_iota(jnp.int32, (TOK, TOK), 0)
    col = lax.broadcasted_iota(jnp.int32, (TOK, TOK), 1)
    before = one_hot(row < col)
    value = lax.broadcasted_iota(jnp.int32, (16, TOK), 0)
    for g in range(3):
        chosen = picks_ref[g : g + 1, :] == value
        rank = jnp.dot(one_hot(chosen), before, preferred_element_type=F32)
        pos = jnp.sum(jnp.where(chosen, rank + 32.0 * value.astype(F32), 0.0), axis=0, keepdims=True)
        pos = pos.astype(jnp.int32)
        pos_ref[g : g + 1, :] = pos
        sel = row == pos
        out_ref[g * TOK : (g + 1) * TOK, : 2 * CH] = jnp.dot(
            one_hot(sel), x_ref[...], preferred_element_type=F32
        ).astype(BF)
        pr = jnp.sum(
            jnp.where(sel, probs_ref[g : g + 1, :].astype(F32), 0.0), axis=1, keepdims=True
        )
        out_ref[g * TOK : (g + 1) * TOK, 2 * CH :] = jnp.broadcast_to(pr, (TOK, 128)).astype(BF)


def second_pick_kernel(core_ref, pos_ref, og_ref, q_ref, after_ref, out_ref, x_ref):
    reorder(og_ref, q_ref, core_ref[0], x_ref, 0)
    row = lax.broadcasted_iota(jnp.int32, (TOK, TOK), 0)
    for g in range(3):
        out_ref[g * TOK : (g + 1) * TOK, :] = jnp.dot(
            one_hot(row == pos_ref[g : g + 1, :]), x_ref[...], preferred_element_type=F32
        ).astype(BF)


def hidden_kernel(own_ref, peer_ref, after_ref, out_ref):
    for k, ref in enumerate((own_ref, peer_ref)):
        gate = ref[:FW, :].astype(F32)
        up = ref[FW:, :].astype(F32)
        out_ref[k * SLOTS : (k + 1) * SLOTS, :] = (gate * jax.nn.sigmoid(gate) * up).T


def order_kernel(core_ref, w_ref, q0_ref, q1_ref, after_ref, out_ref):
    reorder(w_ref, q0_ref, core_ref[0], out_ref, 0)
    reorder(w_ref, q1_ref, core_ref[0], out_ref, 2 * CH)


def partial_grad(par, own_ref, peer_ref, sh_ref, keep_ref, a_ref, b_ref, acc_ref):
    for a in range(0, CH, 128):
        acc_ref[a : a + 128, :] = lax.dot_general(
            own_ref[:, a : a + 128], sh_ref[:SLOTS, :], ROWS_T, preferred_element_type=F32
        ) + lax.dot_general(
            peer_ref[:, a : a + 128], sh_ref[SLOTS:, :], ROWS_T, preferred_element_type=F32
        )
    for k in range(NK):
        keep_ref[80 * k : 80 * (k + 1), :] = acc_ref[
            pl.ds(pl.multiple_of(PART * k + 80 * par, 16), 80), :
        ]
        to_ref = (a_ref, b_ref)[k // 2]
        to_ref[80 * (k % 2) : 80 * (k % 2 + 1), :] = acc_ref[
            pl.ds(pl.multiple_of(PART * k + 80 * (1 - par), 16), 80), :
        ].astype(BF)


def first_grad_kernel(
    par_ref, own_ref, prob_ref, peer_ref, hid_ref, after_ref,
    keep_ref, a_ref, b_ref, sh_ref, acc_ref,
):
    for k, p in enumerate((prob_ref[...], peer_ref[:, CH:])):
        p = p.astype(F32)
        for a in range(0, FW, 128):
            b = min(a + 128, FW)
            sh_ref[k * SLOTS : (k + 1) * SLOTS, a:b] = (
                p[:, : b - a] * hid_ref[k * SLOTS : (k + 1) * SLOTS, a:b]
            ).astype(BF)
    partial_grad(par_ref[0], own_ref, peer_ref, sh_ref, keep_ref, a_ref, b_ref, acc_ref)


def second_grad_kernel(par_ref, own_ref, peer_ref, sh_ref, keep_ref, a_ref, b_ref, acc_ref):
    partial_grad(par_ref[0], own_ref, peer_ref, sh_ref, keep_ref, a_ref, b_ref, acc_ref)


def other_kernel(rows_ref, after_ref, out_ref):
    out_ref[...] = rows_ref[...]


def pair_kernel(keep_ref, a_ref, b_ref, out_ref):
    out_ref[:160, :] = (keep_ref[:160, :] + a_ref[...].astype(F32)).astype(BF)
    out_ref[160:, :] = (keep_ref[160:, :] + b_ref[...].astype(F32)).astype(BF)


def sum_kernel(x0_ref, x1_ref, after_ref, out_ref):
    for k, ref in enumerate((x0_ref, x1_ref)):
        total = ref[0].astype(F32)
        for n in range(1, NK):
            total += ref[n].astype(F32)
        out_ref[80 * k : 80 * (k + 1), :] = total.astype(BF)


def last_kernel(x_ref, out_ref):
    total = x_ref[0].astype(F32)
    for n in range(1, NZ):
        total += x_ref[n].astype(F32)
    out_ref[...] = total


def pre_kernel(w_ref, r0_ref, r1_ref, sp_ref, after_ref, pg_ref, sg_ref):
    lane = lax.broadcasted_iota(jnp.int32, (16, 128), 1)
    prob = lax.dot_general(
        one_hot(lane == 0), r0_ref[:, 2 * CH :], LANES_T, preferred_element_type=F32
    )[:1]
    total = jnp.zeros((1, SLOTS), F32)
    step = FW // 3
    for a in range(0, FW, step):
        proj = lax.dot_general(
            w_ref[a : a + step, : 2 * CH], r0_ref[:, : 2 * CH], LANES_T, preferred_element_type=F32
        ) + lax.dot_general(
            w_ref[a : a + step, 2 * CH :], r1_ref[...], LANES_T, preferred_element_type=F32
        )
        gate = sp_ref[a : a + step, :].astype(F32)
        up = sp_ref[FW + a : FW + a + step, :].astype(F32)
        sig = jax.nn.sigmoid(gate)
        act = gate * sig
        total += jnp.sum(act * up * proj, axis=0, keepdims=True)
        hg = prob * proj
        pg_ref[a : a + step, :] = (hg * up * sig * (1.0 + gate * (1.0 - sig))).astype(BF)
        pg_ref[FW + a : FW + a + step, :] = (hg * act).astype(BF)
    sg_ref[...] = total


def back_kernel(zl_ref, x_ref, picks_ref, pos_ref, every_ref, out_ref):
    zl, x = zl_ref[0], x_ref[0]
    lane = lax.broadcasted_iota(jnp.int32, (SLOTS, TOK), 0)
    row = lax.broadcasted_iota(jnp.int32, (12, TOK), 0)
    for g in range(3):
        pick = picks_ref[g : g + 1, :]
        rank = pos_ref[g : g + 1, :] - 32 * pick
        at = jnp.where(lane == rank + 32 * (NX * zl + x), 1.0, 0.0)
        got = jnp.dot(
            every_ref[...], at, preferred_element_type=F32, precision=lax.Precision.HIGHEST
        )
        back = jnp.where(zl >= g, zl - g, zl - g + NZL)
        from_row = NX * back + ((x - pick + NX) & (NX - 1))
        out_ref[g : g + 1, :] = jnp.sum(jnp.where(row == from_row, got, 0.0), axis=0, keepdims=True)


SMEM = pl.BlockSpec(memory_space=pltpu.SMEM)
AFTER = pl.BlockSpec(memory_space=pl.ANY)


def full(*shape):
    return pl.BlockSpec(shape, lambda i: (0,) * len(shape))


def block(rows, columns, at):
    return pl.BlockSpec((rows, columns), lambda i: (0, at))


def half(chunk):
    return pl.BlockSpec((BLK, 2 * PART), lambda i: (chunk, 0))


def call(kernel, name, outs, in_specs, scratch=(), macs=0, mbytes=4, mib=60):
    shapes = tuple(jax.ShapeDtypeStruct(s, t) for s, t in outs)
    return pl.pallas_call(
        kernel,
        grid=(1,),
        out_shape=shapes,
        in_specs=in_specs,
        out_specs=tuple(full(*s) for s, _ in outs),
        scratch_shapes=[pltpu.VMEM(s, t) for s, t in scratch],
        compiler_params=pltpu.CompilerParams(vmem_limit_bytes=mib * 1024 * 1024),
        cost_estimate=pl.CostEstimate(
            flops=2 * macs, bytes_accessed=mbytes * 1_000_000, transcendentals=0
        ),
        name=name,
    )


def on_device(out_grad, probs, picks, saved_pre, down_weight):
    def scalar(name):
        return lax.axis_index(name).astype(jnp.int32).reshape(1)

    core, par = scalar("c"), scalar("p")
    swap = [(0, 1), (1, 0)]
    up_pair = [(y, y ^ 1) for y in range(8)]
    down_pair = [(y, (y + 1 if y % 2 else y - 1) % 8) for y in range(8)]
    q = jnp.asarray(split_matrices(), BF)
    sp_t = saved_pre.T
    w_t = down_weight[0].T
    picks_t = picks.T

    def dispatch(rows):
        return lax.all_to_all(
            rows.reshape(12, 32, -1), ("zl", "x"), split_axis=0, concat_axis=0, tiled=True
        ).reshape(SLOTS, -1)

    send0, pos = call(
        first_pick_kernel, "first_pick",
        [((SLOTS, 2 * CH + 128), BF), ((3, TOK), jnp.int32)],
        [SMEM, full(3, TOK), full(3, TOK), full(TOK, D), half(0)],
        [((TOK, 2 * CH), BF)], 200_000_000,
    )(core, picks_t, probs.T, out_grad, q)
    recv0 = dispatch(send0)
    (hid,) = call(
        hidden_kernel, "hidden", [((2 * SLOTS, FW), F32)],
        [full(2 * FW, SLOTS), full(2 * FW, SLOTS), AFTER], (), 500_000_000,
    )(sp_t, lax.ppermute(sp_t, "c", swap), pos)
    (w_ord,) = call(
        order_kernel, "order", [((FW, D), BF)],
        [SMEM, full(FW, D), half(0), half(1), AFTER], (), 1_000_000_000, 10,
    )(core, w_t, q, q, hid)
    (send1,) = call(
        second_pick_kernel, "second_pick", [((SLOTS, 2 * CH), BF)],
        [SMEM, full(3, TOK), full(TOK, D), half(1), AFTER],
        [((TOK, 2 * CH), BF)], 200_000_000,
    )(core, pos, out_grad, q, w_ord)
    recv1 = dispatch(send1)

    def pair(keep, a, b):
        a = lax.ppermute(a, ("k", "p"), up_pair)
        b = lax.ppermute(b, ("k", "p"), down_pair)
        (out,) = call(
            pair_kernel, "pair", [((NK * 80, FW), BF)],
            [full(NK * 80, FW), full(160, FW), full(160, FW)], (), 1_000_000, 2, 16,
        )(keep, a, b)
        return out, lax.all_to_all(
            out.reshape(NK, 80, FW), "k", split_axis=0, concat_axis=0, tiled=True
        )

    parts = [((NK * 80, FW), F32), ((160, FW), BF), ((160, FW), BF)]
    peer0 = lax.ppermute(recv0[:, CH:], "c", swap)
    keep0, a0, b0, sh = call(
        first_grad_kernel, "first_grad", [*parts, ((2 * SLOTS, FW), BF)],
        [SMEM, block(SLOTS, CH, 0), block(SLOTS, 128, 2 * CH // 128), full(SLOTS, CH + 128),
         full(2 * SLOTS, FW), AFTER],
        [((CH, FW), F32)], 330_000_000, 6,
    )(par, recv0, recv0, peer0, hid, w_ord)
    half0, got0 = pair(keep0, a0, b0)
    (other1,) = call(
        other_kernel, "other", [((SLOTS, CH), BF)], [block(SLOTS, CH, 1), AFTER], (), 1_000_000, 1,
    )(recv1, half0)
    peer1 = lax.ppermute(other1, "c", swap)
    keep1, a1, b1 = call(
        second_grad_kernel, "second_grad", parts,
        [SMEM, block(SLOTS, CH, 0), full(SLOTS, CH), full(2 * SLOTS, FW)],
        [((CH, FW), F32)], 330_000_000, 6,
    )(par, recv1, peer1, sh)
    _, got1 = pair(keep1, a1, b1)

    pg_t, slot_grad = call(
        pre_kernel, "pre", [((2 * FW, SLOTS), BF), ((1, SLOTS), F32)],
        [full(FW, D), full(SLOTS, 2 * CH + 128), full(SLOTS, 2 * CH), full(2 * FW, SLOTS), AFTER],
        (), 700_000_000, 9,
    )(w_ord, recv0, recv1, sp_t, keep1)
    def ring(n, by):
        return [(i, (i + by) % n) for i in range(n)]

    row = jnp.concatenate(
        [slot_grad] + [lax.ppermute(slot_grad, "x", ring(NX, d)) for d in range(1, NX)], axis=0
    )
    every = jnp.concatenate(
        [row] + [lax.ppermute(row, "zl", ring(NZL, d)) for d in range(1, NZL)], axis=0
    )
    (prob_t,) = call(
        back_kernel, "back", [((3, TOK), F32)],
        [SMEM, SMEM, full(3, TOK), full(3, TOK), full(12, SLOTS)], (), 1_000_000, 1,
    )(scalar("zl"), scalar("x"), picks_t, pos, every)
    (sums,) = call(
        sum_kernel, "sum", [((NZ * OWN, FW), BF)],
        [full(NK, 80, FW), full(NK, 80, FW), AFTER], (), 1_000_000, 2, 16,
    )(got0, got1, prob_t)
    over_z = lax.all_to_all(
        sums.reshape(NZ, OWN, FW), "z", split_axis=0, concat_axis=0, tiled=True
    )
    (down_grad,) = call(
        last_kernel, "last", [((OWN, FW), F32)], [full(NZ, OWN, FW)], (), 1_000_000, 1, 16,
    )(over_z)
    return (pg_t.T, down_grad[None], prob_t.T)


def solution(mesh):
    names = ("k", "p", "z", "c", "zl", "x")
    cut = Mesh(mesh.devices.reshape(NK, NP, NZ, NC, NZL, NX), names)
    rows = P(names, None)
    in_specs = (rows, rows, rows, rows, P(("zl", "x"), None, None))
    out_specs = (rows, P(("zl", "x"), ("k", "p", "z", "c"), None), rows)
    return jax.shard_map(
        on_device, mesh=cut, in_specs=in_specs, out_specs=out_specs, check_vma=False
    )
```

```python
import functools

import jax
import jax.numpy as jnp
import numpy as np
from jax import lax
from jax.experimental import pallas as pl
from jax.experimental.pallas import tpu as pltpu
from jax.sharding import Mesh, PartitionSpec as P

BF = jnp.bfloat16
F32 = jnp.float32
NY, NZ, NC, NZL, NX = 8, 4, 2, 3, 4
D, FW, TOK, SLOTS, OWN = 2560, 672, 128, 384, 40
BLK = D // 4
FIRST = 24
W0, W1 = D // 2 * FIRST // OWN, D // 2 * (OWN - FIRST) // OWN
ROWS_T = (((0,), (0,)), ((), ()))
LANES_T = (((1,), (1,)), ((), ()))


def split_matrix(start, size):
    n = np.arange(16 * size)
    h, y, z, i = n // (8 * size), n // (4 * size) % 2, n // size % 4, n % size
    m = np.zeros((BLK, 16 * size), np.float32)
    m[y * 320 + z * 80 + h * OWN + start + i, n] = 1.0
    return jnp.asarray(m, BF)


def one_hot(mask):
    return jnp.where(mask, 1.0, 0.0).astype(BF)


def reorder(ref, q_ref, core, out_ref, base):
    part = q_ref.shape[1] // 2
    y = [
        jnp.dot(ref[:, BLK * k : BLK * (k + 1)], q_ref[...], preferred_element_type=F32)
        for k in range(4)
    ]
    for h in range(2):
        at = pl.multiple_of((core ^ h) * 4 * part + base, 128)
        out_ref[:, pl.ds(at, 4 * part)] = jnp.concatenate(
            [v[:, part * h : part * (h + 1)] for v in y], axis=1
        ).astype(BF)


def first_pick_kernel(core_ref, picks_ref, probs_ref, og_ref, q_ref, out_ref, pos_ref, x_ref):
    reorder(og_ref, q_ref, core_ref[0], x_ref, 0)
    row = lax.broadcasted_iota(jnp.int32, (TOK, TOK), 0)
    col = lax.broadcasted_iota(jnp.int32, (TOK, TOK), 1)
    before = one_hot(row < col)
    value = lax.broadcasted_iota(jnp.int32, (16, TOK), 0)
    for g in range(3):
        chosen = picks_ref[g : g + 1, :] == value
        rank = jnp.dot(one_hot(chosen), before, preferred_element_type=F32)
        pos = jnp.sum(jnp.where(chosen, rank + 32.0 * value.astype(F32), 0.0), axis=0, keepdims=True)
        pos = pos.astype(jnp.int32)
        pos_ref[g : g + 1, :] = pos
        sel = row == pos
        out_ref[g * TOK : (g + 1) * TOK, : 2 * W0] = jnp.dot(
            one_hot(sel), x_ref[...], preferred_element_type=F32
        ).astype(BF)
        pr = jnp.sum(
            jnp.where(sel, probs_ref[g : g + 1, :].astype(F32), 0.0), axis=1, keepdims=True
        )
        out_ref[g * TOK : (g + 1) * TOK, 2 * W0 :] = jnp.broadcast_to(pr, (TOK, 128)).astype(BF)


def second_pick_kernel(core_ref, pos_ref, og_ref, q_ref, after_ref, out_ref, x_ref):
    reorder(og_ref, q_ref, core_ref[0], x_ref, 0)
    row = lax.broadcasted_iota(jnp.int32, (TOK, TOK), 0)
    for g in range(3):
        out_ref[g * TOK : (g + 1) * TOK, :] = jnp.dot(
            one_hot(row == pos_ref[g : g + 1, :]), x_ref[...], preferred_element_type=F32
        ).astype(BF)


def hidden_kernel(own_ref, peer_ref, after_ref, out_ref):
    for k, ref in enumerate((own_ref, peer_ref)):
        gate = ref[:FW, :].astype(F32)
        up = ref[FW:, :].astype(F32)
        out_ref[k * SLOTS : (k + 1) * SLOTS, :] = (gate * jax.nn.sigmoid(gate) * up).T


def order_kernel(core_ref, w_ref, q0_ref, q1_ref, after_ref, out_ref):
    reorder(w_ref, q0_ref, core_ref[0], out_ref, 0)
    reorder(w_ref, q1_ref, core_ref[0], out_ref, 2 * W0)


def partial_grad(own_ref, peer_ref, sh_ref, out_ref):
    for a in range(0, out_ref.shape[0], 128):
        out_ref[a : a + 128, :] = (
            lax.dot_general(
                own_ref[:, a : a + 128], sh_ref[:SLOTS, :], ROWS_T, preferred_element_type=F32
            )
            + lax.dot_general(
                peer_ref[:, a : a + 128], sh_ref[SLOTS:, :], ROWS_T, preferred_element_type=F32
            )
        ).astype(out_ref.dtype)


def first_grad_kernel(own_ref, prob_ref, peer_ref, hid_ref, out_ref, sh_ref):
    for k, p in enumerate((prob_ref[...], peer_ref[:, W0:])):
        p = p.astype(F32)
        for a in range(0, FW, 128):
            b = min(a + 128, FW)
            sh_ref[k * SLOTS : (k + 1) * SLOTS, a:b] = (
                p[:, : b - a] * hid_ref[k * SLOTS : (k + 1) * SLOTS, a:b]
            ).astype(BF)
    partial_grad(own_ref, peer_ref, sh_ref, out_ref)


def second_grad_kernel(own_ref, peer_ref, sh_ref, out_ref):
    partial_grad(own_ref, peer_ref, sh_ref, out_ref)


def tail_kernel(first, rows_ref, after_ref, out_ref, sem):
    copy = pltpu.make_async_copy(rows_ref.at[:, first:], out_ref, sem)
    copy.start()
    copy.wait()


def gate_kernel(x_ref, after_ref, out_ref):
    out_ref[...] = x_ref[...]


def sum_kernel(x0_ref, x1_ref, after_ref, out_ref):
    total = x1_ref[0].astype(F32)
    for n in range(1, NY):
        total += x1_ref[n].astype(F32)
    rest = OWN - FIRST
    out_ref[...] = jnp.concatenate(
        [
            part
            for z in range(NZ)
            for part in (x0_ref[FIRST * z : FIRST * (z + 1), :], total[rest * z : rest * (z + 1), :])
        ],
        axis=0,
    ).astype(BF)


def last_kernel(x_ref, out_ref):
    total = x_ref[0].astype(F32)
    for n in range(1, NZ):
        total += x_ref[n].astype(F32)
    out_ref[...] = total


def pre_kernel(w_ref, r0_ref, r1_ref, sp_ref, pg_ref, sg_ref):
    lane = lax.broadcasted_iota(jnp.int32, (16, 128), 1)
    prob = lax.dot_general(
        one_hot(lane == 0), r0_ref[:, 2 * W0 :], LANES_T, preferred_element_type=F32
    )[:1]
    total = jnp.zeros((1, SLOTS), F32)
    step = FW // 3
    for a in range(0, FW, step):
        proj = lax.dot_general(
            w_ref[a : a + step, : 2 * W0], r0_ref[:, : 2 * W0], LANES_T, preferred_element_type=F32
        ) + lax.dot_general(
            w_ref[a : a + step, 2 * W0 :], r1_ref[...], LANES_T, preferred_element_type=F32
        )
        gate = sp_ref[a : a + step, :].astype(F32)
        up = sp_ref[FW + a : FW + a + step, :].astype(F32)
        sig = jax.nn.sigmoid(gate)
        act = gate * sig
        total += jnp.sum(act * up * proj, axis=0, keepdims=True)
        hg = prob * proj
        pg_ref[a : a + step, :] = (hg * up * sig * (1.0 + gate * (1.0 - sig))).astype(BF)
        pg_ref[FW + a : FW + a + step, :] = (hg * act).astype(BF)
    sg_ref[...] = total


def back_kernel(pos_ref, ret_ref, out_ref):
    row = lax.broadcasted_iota(jnp.int32, (TOK, TOK), 0)
    for g in range(3):
        at = jnp.where(row == pos_ref[g : g + 1, :], 1.0, 0.0)
        got = jnp.broadcast_to(ret_ref[g : g + 1, :], (8, TOK))
        out_ref[g : g + 1, :] = jnp.dot(
            got, at, preferred_element_type=F32, precision=lax.Precision.HIGHEST
        )[:1]


SMEM = pl.BlockSpec(memory_space=pltpu.SMEM)
AFTER = pl.BlockSpec(memory_space=pl.ANY)


def full(*shape):
    return pl.BlockSpec(shape, lambda i: (0,) * len(shape))


def block(rows, columns, at):
    return pl.BlockSpec((rows, columns), lambda i: (0, at))


def call(kernel, name, outs, in_specs, scratch=(), macs=0, mbytes=4, mib=63):
    shapes = tuple(jax.ShapeDtypeStruct(s, t) for s, t in outs)
    return pl.pallas_call(
        kernel,
        grid=(1,),
        out_shape=shapes,
        in_specs=in_specs,
        out_specs=tuple(full(*s) for s, _ in outs),
        scratch_shapes=[pltpu.VMEM(s, t) for s, t in scratch],
        compiler_params=pltpu.CompilerParams(vmem_limit_bytes=mib * 1024 * 1024),
        cost_estimate=pl.CostEstimate(
            flops=2 * macs, bytes_accessed=mbytes * 1_000_000, transcendentals=0
        ),
        name=name,
    )


def tail(rows, first, after):
    return pl.pallas_call(
        functools.partial(tail_kernel, first),
        out_shape=jax.ShapeDtypeStruct((rows.shape[0], rows.shape[1] - first), rows.dtype),
        in_specs=[AFTER, AFTER],
        out_specs=AFTER,
        scratch_shapes=[pltpu.SemaphoreType.DMA],
        compiler_params=pltpu.CompilerParams(vmem_limit_bytes=63 * 1024 * 1024),
        name="tail",
    )(rows, after)


def on_device(out_grad, probs, picks, saved_pre, down_weight):
    core = lax.axis_index("c").astype(jnp.int32).reshape(1)
    swap = [(0, 1), (1, 0)]
    q0, q1 = split_matrix(0, FIRST), split_matrix(FIRST, OWN - FIRST)
    sp_t = saved_pre.T
    w_t = down_weight[0].T

    def exchange(blocks, axes):
        return lax.all_to_all(blocks, axes, split_axis=0, concat_axis=0, tiled=True)

    def dispatch(rows):
        return exchange(rows.reshape(12, 32, -1), ("zl", "x")).reshape(SLOTS, -1)

    send0, pos = call(
        first_pick_kernel, "first_pick",
        [((SLOTS, 2 * W0 + 128), BF), ((3, TOK), jnp.int32)],
        [SMEM, full(3, TOK), full(3, TOK), full(TOK, D), full(*q0.shape)],
        [((TOK, 2 * W0), BF)], 200_000_000,
    )(core, picks.T, probs.T, out_grad, q0)
    recv0 = dispatch(send0)
    (hid,) = call(
        hidden_kernel, "hidden", [((2 * SLOTS, FW), F32)],
        [full(2 * FW, SLOTS), full(2 * FW, SLOTS), AFTER], (), 500_000_000,
    )(sp_t, lax.ppermute(sp_t, "c", swap), pos)
    (send1,) = call(
        second_pick_kernel, "second_pick", [((SLOTS, 2 * W1), BF)],
        [SMEM, full(3, TOK), full(TOK, D), full(*q1.shape), AFTER],
        [((TOK, 2 * W1), BF)], 200_000_000,
    )(core, pos, out_grad, q1, hid)
    recv1 = dispatch(send1)

    peer0 = lax.ppermute(tail(recv0, W0, send1), "c", swap)
    part0, sh = call(
        first_grad_kernel, "first_grad",
        [((W0, FW), F32), ((2 * SLOTS, FW), BF)],
        [block(SLOTS, W0, 0), block(SLOTS, 128, 2 * W0 // 128), full(SLOTS, W0 + 128),
         full(2 * SLOTS, FW)],
        (), 400_000_000, 6,
    )(recv0, recv0, peer0, hid)
    sum0 = lax.psum_scatter(part0, "y", scatter_dimension=0, tiled=True)
    peer1 = lax.ppermute(tail(recv1, W1, part0), "c", swap)
    (part1,) = call(
        second_grad_kernel, "second_grad", [((W1, FW), BF)],
        [block(SLOTS, W1, 0), full(SLOTS, W1), full(2 * SLOTS, FW)], (), 10_000_000_000, 4,
    )(recv1, peer1, sh)
    got1 = exchange(part1.reshape(NY, W1 // NY, FW), "y")

    (w_ord,) = call(
        order_kernel, "order", [((FW, D), BF)],
        [SMEM, full(FW, D), full(*q0.shape), full(*q1.shape), AFTER], (), 1_000_000_000, 10,
    )(core, w_t, q0, q1, part1)
    pg_t, slot_grad = call(
        pre_kernel, "pre", [((2 * FW, SLOTS), BF), ((1, SLOTS), F32)],
        [full(FW, D), full(SLOTS, 2 * W0 + 128), full(SLOTS, 2 * W1), full(2 * FW, SLOTS)],
        (), 700_000_000, 9,
    )(w_ord, recv0, recv1, sp_t)
    (gated,) = call(
        gate_kernel, "gate", [((1, SLOTS), F32)], [full(1, SLOTS), AFTER], (), 1_000_000, 1,
    )(slot_grad, got1)
    ret = exchange(gated.reshape(12, 32), ("zl", "x"))
    (prob_t,) = call(
        back_kernel, "back", [((3, TOK), F32)], [full(3, TOK), full(3, TOK)], (), 1_000_000, 1,
    )(pos, ret.reshape(3, TOK))
    (sums,) = call(
        sum_kernel, "sum", [((NZ * OWN, FW), BF)],
        [full(W0 // NY, FW), full(NY, W1 // NY, FW), AFTER], (), 1_000_000, 2, 16,
    )(sum0, got1, prob_t)
    over_z = exchange(sums.reshape(NZ, OWN, FW), "z")
    (down_grad,) = call(
        last_kernel, "last", [((OWN, FW), F32)], [full(NZ, OWN, FW)], (), 1_000_000, 1, 16,
    )(over_z)
    return (pg_t.T, down_grad[None], prob_t.T)


def solution(mesh):
    names = ("y", "z", "c", "zl", "x")
    cut = Mesh(mesh.devices.reshape(NY, NZ, NC, NZL, NX), names)
    rows = P(names, None)
    in_specs = (rows, rows, rows, rows, P(("zl", "x"), None, None))
    out_specs = (rows, P(("zl", "x"), ("y", "z", "c"), None), rows)
    return jax.shard_map(
        on_device, mesh=cut, in_specs=in_specs, out_specs=out_specs, check_vma=False
    )
```

```python
import jax
import jax.numpy as jnp
import numpy as np
from jax import lax
from jax.experimental import pallas as pl
from jax.experimental.pallas import tpu as pltpu
from jax.sharding import Mesh, PartitionSpec as P

BF = jnp.bfloat16
F32 = jnp.float32
NY, NZ, NC, NZL, NX = 8, 4, 2, 3, 4
D, FW, TOK, SLOTS, OWN = 2560, 672, 128, 384, 40
BLK = D // 4
FIRST = 24
W0, W1 = D // 2 * FIRST // OWN, D // 2 * (OWN - FIRST) // OWN
R0, R1 = W0 // NY, W1 // NY
ROWS_T = (((0,), (0,)), ((), ()))
LANES_T = (((1,), (1,)), ((), ()))


def split_matrix(start, size):
    n = np.arange(16 * size)
    h, y, z, i = n // (8 * size), n // (4 * size) % 2, n // size % 4, n % size
    m = np.zeros((BLK, 16 * size), np.float32)
    m[y * 320 + z * 80 + h * OWN + start + i, n] = 1.0
    return jnp.asarray(m, BF)


def one_hot(mask):
    return jnp.where(mask, 1.0, 0.0).astype(BF)


def reorder(ref, q_ref, core, out_ref, base):
    part = q_ref.shape[1] // 2
    y = [
        jnp.dot(ref[:, BLK * k : BLK * (k + 1)], q_ref[...], preferred_element_type=F32)
        for k in range(4)
    ]
    for h in range(2):
        at = pl.multiple_of((core ^ h) * 4 * part + base, 128)
        out_ref[:, pl.ds(at, 4 * part)] = jnp.concatenate(
            [v[:, part * h : part * (h + 1)] for v in y], axis=1
        ).astype(BF)


def first_pick_kernel(core_ref, picks_ref, probs_ref, og_ref, q_ref, out_ref, pos_ref, x_ref):
    reorder(og_ref, q_ref, core_ref[0], x_ref, 0)
    row = lax.broadcasted_iota(jnp.int32, (TOK, TOK), 0)
    col = lax.broadcasted_iota(jnp.int32, (TOK, TOK), 1)
    before = one_hot(row < col)
    value = lax.broadcasted_iota(jnp.int32, (16, TOK), 0)
    for g in range(3):
        chosen = picks_ref[g : g + 1, :] == value
        rank = jnp.dot(one_hot(chosen), before, preferred_element_type=F32)
        pos = jnp.sum(jnp.where(chosen, rank + 32.0 * value.astype(F32), 0.0), axis=0, keepdims=True)
        pos = pos.astype(jnp.int32)
        pos_ref[g : g + 1, :] = pos
        sel = row == pos
        out_ref[g * TOK : (g + 1) * TOK, : 2 * W0] = jnp.dot(
            one_hot(sel), x_ref[...], preferred_element_type=F32
        ).astype(BF)
        pr = jnp.sum(
            jnp.where(sel, probs_ref[g : g + 1, :].astype(F32), 0.0), axis=1, keepdims=True
        )
        out_ref[g * TOK : (g + 1) * TOK, 2 * W0 :] = jnp.broadcast_to(pr, (TOK, 128)).astype(BF)


def second_pick_kernel(core_ref, pos_ref, og_ref, q_ref, after_ref, out_ref, x_ref):
    reorder(og_ref, q_ref, core_ref[0], x_ref, 0)
    row = lax.broadcasted_iota(jnp.int32, (TOK, TOK), 0)
    for g in range(3):
        out_ref[g * TOK : (g + 1) * TOK, :] = jnp.dot(
            one_hot(row == pos_ref[g : g + 1, :]), x_ref[...], preferred_element_type=F32
        ).astype(BF)


def hidden_kernel(own_ref, peer_ref, after_ref, out_ref):
    for k, ref in enumerate((own_ref, peer_ref)):
        gate = ref[:FW, :].astype(F32)
        up = ref[FW:, :].astype(F32)
        out_ref[k * SLOTS : (k + 1) * SLOTS, :] = (gate * jax.nn.sigmoid(gate) * up).T


def order_kernel(core_ref, w_ref, q0_ref, q1_ref, after_ref, out_ref):
    reorder(w_ref, q0_ref, core_ref[0], out_ref, 0)
    reorder(w_ref, q1_ref, core_ref[0], out_ref, 2 * W0)


def partial_grad(own_ref, peer_ref, sh_ref, out_ref, acc_ref):
    rows = acc_ref.shape[0] // NY
    quarter = rows // 4
    for a in range(0, acc_ref.shape[0], 128):
        acc_ref[a : a + 128, :] = lax.dot_general(
            own_ref[:, a : a + 128], sh_ref[:SLOTS, :], ROWS_T, preferred_element_type=F32
        ) + lax.dot_general(
            peer_ref[:, a : a + 128], sh_ref[SLOTS:, :], ROWS_T, preferred_element_type=F32
        )
    for y in range(NY):
        for j in range(5):
            out_ref[y, rows * j : rows * (j + 1), :] = acc_ref[
                rows * y : rows * (y + 1), 128 * j : 128 * (j + 1)
            ].astype(BF)
        last = jnp.concatenate(
            [
                acc_ref[rows * y + quarter * n : rows * y + quarter * (n + 1), 640:]
                for n in range(4)
            ],
            axis=1,
        )
        fill = out_ref.shape[1] - 5 * rows - quarter
        if fill:
            last = jnp.concatenate([last, jnp.zeros((fill, 128), F32)], axis=0)
        out_ref[y, 5 * rows :, :] = last.astype(BF)


def first_grad_kernel(own_ref, prob_ref, peer_ref, hid_ref, out_ref, sh_ref, acc_ref):
    for k, p in enumerate((prob_ref[...], peer_ref[:, W0:])):
        p = p.astype(F32)
        for a in range(0, FW, 128):
            b = min(a + 128, FW)
            sh_ref[k * SLOTS : (k + 1) * SLOTS, a:b] = (
                p[:, : b - a] * hid_ref[k * SLOTS : (k + 1) * SLOTS, a:b]
            ).astype(BF)
    partial_grad(own_ref, peer_ref, sh_ref, out_ref, acc_ref)


def second_grad_kernel(own_ref, peer_ref, sh_ref, after_ref, out_ref, acc_ref):
    partial_grad(own_ref, peer_ref, sh_ref, out_ref, acc_ref)


def tail_kernel(rows_ref, after_ref, out_ref):
    out_ref[...] = rows_ref[:, rows_ref.shape[1] - out_ref.shape[1] :]


def gate_kernel(x_ref, after_ref, out_ref):
    pass


def unpacked_sum(ref, rows):
    total = ref[0].astype(F32)
    for n in range(1, NY):
        total += ref[n].astype(F32)
    last = total[5 * rows : 5 * rows + rows // 4]
    return jnp.concatenate(
        [total[rows * j : rows * (j + 1)] for j in range(5)]
        + [jnp.concatenate([last[:, 32 * n : 32 * (n + 1)] for n in range(4)], axis=0)],
        axis=1,
    )


def sum_kernel(x0_ref, x1_ref, after_ref, out_ref):
    x0, x1 = unpacked_sum(x0_ref, R0), unpacked_sum(x1_ref, R1)
    out_ref[...] = jnp.concatenate(
        [part[n * z : n * (z + 1)] for z in range(NZ) for part, n in ((x0, R0 // NZ), (x1, R1 // NZ))],
        axis=0,
    ).astype(BF)


def last_kernel(x_ref, out_ref):
    total = x_ref[0].astype(F32)
    for n in range(1, NZ):
        total += x_ref[n].astype(F32)
    out_ref[...] = total


def pre_kernel(w_ref, r0_ref, r1_ref, gate_ref, up_ref, pg_ref, sg_ref):
    lane = lax.broadcasted_iota(jnp.int32, (16, 128), 1)
    prob = lax.dot_general(
        one_hot(lane == 0), r0_ref[:, 2 * W0 :], LANES_T, preferred_element_type=F32
    )[:1]
    proj = lax.dot_general(
        w_ref[:, : 2 * W0], r0_ref[:, : 2 * W0], LANES_T, preferred_element_type=F32
    ) + lax.dot_general(w_ref[:, 2 * W0 :], r1_ref[...], LANES_T, preferred_element_type=F32)
    gate = gate_ref[...].astype(F32)
    up = up_ref[...].astype(F32)
    sig = jax.nn.sigmoid(gate)
    act = gate * sig
    part = jnp.sum(act * up * proj, axis=0, keepdims=True)
    sg_ref[...] = jnp.where(pl.program_id(0) == 0, part, part + sg_ref[...])
    hg = prob * proj
    pg_ref[0] = (hg * up * sig * (1.0 + gate * (1.0 - sig))).astype(BF)
    pg_ref[1] = (hg * act).astype(BF)


def back_kernel(zl_ref, x_ref, picks_ref, pos_ref, every_ref, out_ref):
    zl, x = zl_ref[0], x_ref[0]
    lane = lax.broadcasted_iota(jnp.int32, (SLOTS, TOK), 0)
    row = lax.broadcasted_iota(jnp.int32, (12, TOK), 0)
    for g in range(3):
        pick = picks_ref[g : g + 1, :]
        rank = pos_ref[g : g + 1, :] - 32 * pick
        at = jnp.where(lane == rank + 32 * (NX * zl + x), 1.0, 0.0)
        got = jnp.dot(
            every_ref[...], at, preferred_element_type=F32, precision=lax.Precision.HIGHEST
        )
        back = jnp.where(zl >= g, zl - g, zl - g + NZL)
        from_row = NX * back + ((x - pick + NX) & (NX - 1))
        out_ref[g : g + 1, :] = jnp.sum(jnp.where(row == from_row, got, 0.0), axis=0, keepdims=True)


SMEM = pl.BlockSpec(memory_space=pltpu.SMEM)
AFTER = pl.BlockSpec(memory_space=pl.ANY)


def full(*shape):
    return pl.BlockSpec(shape, lambda i: (0,) * len(shape))


def block(rows, columns, at):
    return pl.BlockSpec((rows, columns), lambda i: (0, at))


def call(kernel, name, outs, in_specs, scratch=(), macs=0, mbytes=4, mib=63, steps=1, out_specs=None):
    shapes = tuple(jax.ShapeDtypeStruct(s, t) for s, t in outs)
    return pl.pallas_call(
        kernel,
        grid=(steps,),
        out_shape=shapes,
        in_specs=in_specs,
        out_specs=out_specs or tuple(full(*s) for s, _ in outs),
        scratch_shapes=[pltpu.VMEM(s, t) for s, t in scratch],
        compiler_params=pltpu.CompilerParams(vmem_limit_bytes=mib * 1024 * 1024),
        cost_estimate=pl.CostEstimate(
            flops=2 * macs, bytes_accessed=mbytes * 1_000_000, transcendentals=0
        ),
        name=name,
    )


def on_device(out_grad, probs, picks, saved_pre, down_weight):
    def scalar(name):
        return lax.axis_index(name).astype(jnp.int32).reshape(1)

    core = scalar("c")
    swap = [(0, 1), (1, 0)]
    q0, q1 = split_matrix(0, FIRST), split_matrix(FIRST, OWN - FIRST)
    sp_t = saved_pre.T
    w_t = down_weight[0].T

    def exchange(blocks, axes):
        return lax.all_to_all(blocks, axes, split_axis=0, concat_axis=0, tiled=True)

    def dispatch(rows):
        return exchange(rows.reshape(12, 32, -1), ("zl", "x")).reshape(SLOTS, -1)

    send0, pos = call(
        first_pick_kernel, "first_pick",
        [((SLOTS, 2 * W0 + 128), BF), ((3, TOK), jnp.int32)],
        [SMEM, full(3, TOK), full(3, TOK), full(TOK, D), full(*q0.shape)],
        [((TOK, 2 * W0), BF)], 200_000_000,
    )(core, picks.T, probs.T, out_grad, q0)
    recv0 = dispatch(send0)
    (hid,) = call(
        hidden_kernel, "hidden", [((2 * SLOTS, FW), F32)],
        [full(2 * FW, SLOTS), full(2 * FW, SLOTS), AFTER], (), 500_000_000,
    )(sp_t, lax.ppermute(sp_t, "c", swap), pos)
    (w_ord,) = call(
        order_kernel, "order", [((FW, D), BF)],
        [SMEM, pl.BlockSpec((FW // 3, D), lambda i: (i, 0)), full(*q0.shape), full(*q1.shape), AFTER],
        (), 1_000_000_000, 10, 63, 3, (pl.BlockSpec((FW // 3, D), lambda i: (i, 0)),),
    )(core, w_t, q0, q1, hid)
    (send1,) = call(
        second_pick_kernel, "second_pick", [((SLOTS, 2 * W1), BF)],
        [SMEM, full(3, TOK), full(TOK, D), full(*q1.shape), AFTER],
        [((TOK, 2 * W1), BF)], 200_000_000,
    )(core, pos, out_grad, q1, w_ord)
    recv1 = dispatch(send1)

    def tail(rows, width, after):
        size = rows.shape[1] - width
        (out,) = call(
            tail_kernel, "tail", [((SLOTS, size), BF)],
            [full(*rows.shape), AFTER], (), 1_000_000, 1,
        )(rows, after)
        return lax.ppermute(out, "c", swap)

    peer0 = tail(recv0, W0, send1)
    part0, sh = call(
        first_grad_kernel, "first_grad",
        [((NY, 512, 128), BF), ((2 * SLOTS, FW), BF)],
        [block(SLOTS, W0, 0), block(SLOTS, 128, 2 * W0 // 128), full(SLOTS, W0 + 128),
         full(2 * SLOTS, FW)],
        [((W0, FW), F32)], 400_000_000, 6,
    )(recv0, recv0, peer0, hid)
    got0 = exchange(part0, "y")
    peer1 = tail(recv1, W1, part0)
    third = FW // 3
    pg_t, slot_grad = call(
        pre_kernel, "pre", [((2, FW, SLOTS), BF), ((1, SLOTS), F32)],
        [pl.BlockSpec((third, D), lambda i: (i, 0)), full(SLOTS, 2 * W0 + 128), full(SLOTS, 2 * W1),
         pl.BlockSpec((third, SLOTS), lambda i: (i, 0)),
         pl.BlockSpec((third, SLOTS), lambda i: (3 + i, 0))],
        (), 700_000_000, 9, 63, 3,
        (pl.BlockSpec((2, third, SLOTS), lambda i: (0, i, 0)), full(1, SLOTS)),
    )(w_ord, recv0, recv1, sp_t, sp_t)
    (part1,) = call(
        second_grad_kernel, "second_grad", [((NY, 336, 128), BF)],
        [block(SLOTS, W1, 0), full(SLOTS, W1), full(2 * SLOTS, FW), AFTER],
        [((W1, FW), F32)], 270_000_000, 4,
    )(recv1, peer1, sh, slot_grad)
    part1 = pl.pallas_call(
        gate_kernel,
        out_shape=jax.ShapeDtypeStruct(part1.shape, part1.dtype),
        in_specs=[AFTER, AFTER],
        out_specs=AFTER,
        input_output_aliases={0: 0},
        compiler_params=pltpu.CompilerParams(vmem_limit_bytes=63 * 1024 * 1024),
        name="gate",
    )(part1, got0)
    got1 = exchange(part1, "y")

    def ring(n, by):
        return [(i, (i + by) % n) for i in range(n)]

    row = jnp.concatenate(
        [slot_grad] + [lax.ppermute(slot_grad, "x", ring(NX, d)) for d in range(1, NX)], axis=0
    )
    every = jnp.concatenate(
        [row] + [lax.ppermute(row, "zl", ring(NZL, d)) for d in range(1, NZL)], axis=0
    )
    (prob_t,) = call(
        back_kernel, "back", [((3, TOK), F32)],
        [SMEM, SMEM, full(3, TOK), full(3, TOK), full(12, SLOTS)], (), 1_000_000, 1,
    )(scalar("zl"), scalar("x"), picks.T, pos, every)
    (sums,) = call(
        sum_kernel, "sum", [((NZ * OWN, FW), BF)],
        [full(NY, 512, 128), full(NY, 336, 128), AFTER], (), 1_000_000, 2, 16,
    )(got0, got1, row)
    over_z = exchange(sums.reshape(NZ, OWN, FW), "z")
    (down_grad,) = call(
        last_kernel, "last", [((OWN, FW), F32)], [full(NZ, OWN, FW)], (), 1_000_000, 1, 16,
    )(over_z)
    return (pg_t.reshape(2 * FW, SLOTS).T, down_grad[None], prob_t.T)


def solution(mesh):
    names = ("y", "z", "c", "zl", "x")
    cut = Mesh(mesh.devices.reshape(NY, NZ, NC, NZL, NX), names)
    rows = P(names, None)
    in_specs = (rows, rows, rows, rows, P(("zl", "x"), None, None))
    out_specs = (rows, P(("zl", "x"), ("y", "z", "c"), None), rows)
    return jax.shard_map(
        on_device, mesh=cut, in_specs=in_specs, out_specs=out_specs, check_vma=False
    )
```

```python
import jax
import jax.numpy as jnp
import numpy as np
from jax import lax
from jax.experimental import pallas as pl
from jax.experimental.pallas import tpu as pltpu
from jax.sharding import Mesh, PartitionSpec as P

BF = jnp.bfloat16
F32 = jnp.float32
NY, NZ, NC, NZL, NX = 8, 4, 2, 3, 4
D, FW, TOK, SLOTS, OWN = 2560, 672, 128, 384, 40
BLK = D // 4
FIRST = 24
W0, W1 = D // 2 * FIRST // OWN, D // 2 * (OWN - FIRST) // OWN
R0, R1 = W0 // NY, W1 // NY
ROWS_T = (((0,), (0,)), ((), ()))
LANES_T = (((1,), (1,)), ((), ()))


def split_matrix(start, size):
    n = np.arange(16 * size)
    h, y, z, i = n // (8 * size), n // (4 * size) % 2, n // size % 4, n % size
    m = np.zeros((BLK, 16 * size), np.float32)
    m[y * 320 + z * 80 + h * OWN + start + i, n] = 1.0
    return jnp.asarray(m, BF)


def one_hot(mask):
    return jnp.where(mask, 1.0, 0.0).astype(BF)


def reorder(ref, q_ref, core, out_ref, base):
    part = q_ref.shape[1] // 2
    y = [
        jnp.dot(ref[:, BLK * k : BLK * (k + 1)], q_ref[...], preferred_element_type=F32)
        for k in range(4)
    ]
    for h in range(2):
        at = pl.multiple_of((core ^ h) * 4 * part + base, 128)
        out_ref[:, pl.ds(at, 4 * part)] = jnp.concatenate(
            [v[:, part * h : part * (h + 1)] for v in y], axis=1
        ).astype(BF)


def first_pick_kernel(core_ref, picks_ref, probs_ref, og_ref, q_ref, out_ref, pos_ref, x_ref):
    reorder(og_ref, q_ref, core_ref[0], x_ref, 0)
    row = lax.broadcasted_iota(jnp.int32, (TOK, TOK), 0)
    col = lax.broadcasted_iota(jnp.int32, (TOK, TOK), 1)
    before = one_hot(row < col)
    value = lax.broadcasted_iota(jnp.int32, (16, TOK), 0)
    for g in range(3):
        chosen = picks_ref[g : g + 1, :] == value
        rank = jnp.dot(one_hot(chosen), before, preferred_element_type=F32)
        pos = jnp.sum(jnp.where(chosen, rank + 32.0 * value.astype(F32), 0.0), axis=0, keepdims=True)
        pos = pos.astype(jnp.int32)
        pos_ref[g : g + 1, :] = pos
        sel = row == pos
        out_ref[g * TOK : (g + 1) * TOK, : 2 * W0] = jnp.dot(
            one_hot(sel), x_ref[...], preferred_element_type=F32
        ).astype(BF)
        pr = jnp.sum(
            jnp.where(sel, probs_ref[g : g + 1, :].astype(F32), 0.0), axis=1, keepdims=True
        )
        out_ref[g * TOK : (g + 1) * TOK, 2 * W0 :] = jnp.broadcast_to(pr, (TOK, 128)).astype(BF)


def second_pick_kernel(core_ref, pos_ref, og_ref, q_ref, after_ref, out_ref, x_ref):
    reorder(og_ref, q_ref, core_ref[0], x_ref, 0)
    row = lax.broadcasted_iota(jnp.int32, (TOK, TOK), 0)
    for g in range(3):
        out_ref[g * TOK : (g + 1) * TOK, :] = jnp.dot(
            one_hot(row == pos_ref[g : g + 1, :]), x_ref[...], preferred_element_type=F32
        ).astype(BF)


def hidden_kernel(own_ref, peer_ref, after_ref, out_ref):
    for k, ref in enumerate((own_ref, peer_ref)):
        gate = ref[:FW, :].astype(F32)
        up = ref[FW:, :].astype(F32)
        out_ref[k * SLOTS : (k + 1) * SLOTS, :] = (gate * jax.nn.sigmoid(gate) * up).T


def order_kernel(core_ref, w_ref, q0_ref, q1_ref, after_ref, out_ref):
    reorder(w_ref, q0_ref, core_ref[0], out_ref, 0)
    reorder(w_ref, q1_ref, core_ref[0], out_ref, 2 * W0)


def partial_grad(own_ref, peer_ref, sh_ref, out_ref, acc_ref):
    rows = acc_ref.shape[0] // NY
    quarter = rows // 4
    for a in range(0, acc_ref.shape[0], 128):
        acc_ref[a : a + 128, :] = lax.dot_general(
            own_ref[:, a : a + 128], sh_ref[:SLOTS, :], ROWS_T, preferred_element_type=F32
        ) + lax.dot_general(
            peer_ref[:, a : a + 128], sh_ref[SLOTS:, :], ROWS_T, preferred_element_type=F32
        )
    for y in range(NY):
        for j in range(5):
            out_ref[y, rows * j : rows * (j + 1), :] = acc_ref[
                rows * y : rows * (y + 1), 128 * j : 128 * (j + 1)
            ].astype(BF)
        last = jnp.concatenate(
            [
                acc_ref[rows * y + quarter * n : rows * y + quarter * (n + 1), 640:]
                for n in range(4)
            ],
            axis=1,
        )
        fill = out_ref.shape[1] - 5 * rows - quarter
        if fill:
            last = jnp.concatenate([last, jnp.zeros((fill, 128), F32)], axis=0)
        out_ref[y, 5 * rows :, :] = last.astype(BF)


def first_grad_kernel(own_ref, prob_ref, peer_ref, hid_ref, out_ref, sh_ref, acc_ref):
    for k, p in enumerate((prob_ref[...], peer_ref[:, W0:])):
        p = p.astype(F32)
        for a in range(0, FW, 128):
            b = min(a + 128, FW)
            sh_ref[k * SLOTS : (k + 1) * SLOTS, a:b] = (
                p[:, : b - a] * hid_ref[k * SLOTS : (k + 1) * SLOTS, a:b]
            ).astype(BF)
    partial_grad(own_ref, peer_ref, sh_ref, out_ref, acc_ref)


def second_grad_kernel(own_ref, peer_ref, sh_ref, after_ref, out_ref, acc_ref):
    partial_grad(own_ref, peer_ref, sh_ref, out_ref, acc_ref)


def tail_kernel(rows_ref, after_ref, out_ref):
    out_ref[...] = rows_ref[:, rows_ref.shape[1] - out_ref.shape[1] :]


def gate_kernel(x_ref, blocks_ref, row_ref, out_ref):
    pass


def unpacked_sum(ref, rows):
    total = ref[0].astype(F32)
    for n in range(1, NY):
        total += ref[n].astype(F32)
    last = total[5 * rows : 5 * rows + rows // 4]
    return jnp.concatenate(
        [total[rows * j : rows * (j + 1)] for j in range(5)]
        + [jnp.concatenate([last[:, 32 * n : 32 * (n + 1)] for n in range(4)], axis=0)],
        axis=1,
    )


def sum_kernel(x0_ref, x1_ref, after_ref, out_ref):
    x0, x1 = unpacked_sum(x0_ref, R0), unpacked_sum(x1_ref, R1)
    out_ref[...] = jnp.concatenate(
        [part[n * z : n * (z + 1)] for z in range(NZ) for part, n in ((x0, R0 // NZ), (x1, R1 // NZ))],
        axis=0,
    ).astype(BF)


def last_kernel(x_ref, out_ref):
    total = x_ref[0].astype(F32)
    for n in range(1, NZ):
        total += x_ref[n].astype(F32)
    out_ref[...] = total


def pre_kernel(w_ref, r0_ref, r1_ref, gate_ref, up_ref, pg_ref, sg_ref):
    lane = lax.broadcasted_iota(jnp.int32, (16, 128), 1)
    prob = lax.dot_general(
        one_hot(lane == 0), r0_ref[:, 2 * W0 :], LANES_T, preferred_element_type=F32
    )[:1]
    proj = lax.dot_general(
        w_ref[:, : 2 * W0], r0_ref[:, : 2 * W0], LANES_T, preferred_element_type=F32
    ) + lax.dot_general(w_ref[:, 2 * W0 :], r1_ref[...], LANES_T, preferred_element_type=F32)
    gate = gate_ref[...].astype(F32)
    up = up_ref[...].astype(F32)
    sig = jax.nn.sigmoid(gate)
    act = gate * sig
    part = jnp.sum(act * up * proj, axis=0, keepdims=True)
    sg_ref[...] = jnp.where(pl.program_id(0) == 0, part, part + sg_ref[...])
    hg = prob * proj
    pg_ref[0] = (hg * up * sig * (1.0 + gate * (1.0 - sig))).astype(BF)
    pg_ref[1] = (hg * act).astype(BF)


def back_kernel(zl_ref, x_ref, picks_ref, pos_ref, every_ref, out_ref):
    zl, x = zl_ref[0], x_ref[0]
    lane = lax.broadcasted_iota(jnp.int32, (SLOTS, TOK), 0)
    row = lax.broadcasted_iota(jnp.int32, (12, TOK), 0)
    for g in range(3):
        pick = picks_ref[g : g + 1, :]
        rank = pos_ref[g : g + 1, :] - 32 * pick
        at = jnp.where(lane == rank + 32 * (NX * zl + x), 1.0, 0.0)
        got = jnp.dot(
            every_ref[...], at, preferred_element_type=F32, precision=lax.Precision.HIGHEST
        )
        back = jnp.where(zl >= g, zl - g, zl - g + NZL)
        from_row = NX * back + ((x - pick + NX) & (NX - 1))
        out_ref[g : g + 1, :] = jnp.sum(jnp.where(row == from_row, got, 0.0), axis=0, keepdims=True)


SMEM = pl.BlockSpec(memory_space=pltpu.SMEM)
AFTER = pl.BlockSpec(memory_space=pl.ANY)


def full(*shape):
    return pl.BlockSpec(shape, lambda i: (0,) * len(shape))


def block(rows, columns, at):
    return pl.BlockSpec((rows, columns), lambda i: (0, at))


def call(kernel, name, outs, in_specs, scratch=(), macs=0, mbytes=4, mib=63, steps=1, out_specs=None):
    shapes = tuple(jax.ShapeDtypeStruct(s, t) for s, t in outs)
    return pl.pallas_call(
        kernel,
        grid=(steps,),
        out_shape=shapes,
        in_specs=in_specs,
        out_specs=out_specs or tuple(full(*s) for s, _ in outs),
        scratch_shapes=[pltpu.VMEM(s, t) for s, t in scratch],
        compiler_params=pltpu.CompilerParams(vmem_limit_bytes=mib * 1024 * 1024),
        cost_estimate=pl.CostEstimate(
            flops=2 * macs, bytes_accessed=mbytes * 1_000_000, transcendentals=0
        ),
        name=name,
    )


def on_device(out_grad, probs, picks, saved_pre, down_weight):
    def scalar(name):
        return lax.axis_index(name).astype(jnp.int32).reshape(1)

    core = scalar("c")
    swap = [(0, 1), (1, 0)]
    q0, q1 = split_matrix(0, FIRST), split_matrix(FIRST, OWN - FIRST)
    sp_t = saved_pre.T
    w_t = down_weight[0].T

    def exchange(blocks, axes):
        return lax.all_to_all(blocks, axes, split_axis=0, concat_axis=0, tiled=True)

    def dispatch(rows):
        return exchange(rows.reshape(12, 32, -1), ("zl", "x")).reshape(SLOTS, -1)

    send0, pos = call(
        first_pick_kernel, "first_pick",
        [((SLOTS, 2 * W0 + 128), BF), ((3, TOK), jnp.int32)],
        [SMEM, full(3, TOK), full(3, TOK), full(TOK, D), full(*q0.shape)],
        [((TOK, 2 * W0), BF)], 200_000_000,
    )(core, picks.T, probs.T, out_grad, q0)
    recv0 = dispatch(send0)
    (hid,) = call(
        hidden_kernel, "hidden", [((2 * SLOTS, FW), F32)],
        [full(2 * FW, SLOTS), full(2 * FW, SLOTS), AFTER], (), 500_000_000,
    )(sp_t, lax.ppermute(sp_t, "c", swap), pos)
    (w_ord,) = call(
        order_kernel, "order", [((FW, D), BF)],
        [SMEM, pl.BlockSpec((FW // 3, D), lambda i: (i, 0)), full(*q0.shape), full(*q1.shape), AFTER],
        (), 1_000_000_000, 10, 63, 3, (pl.BlockSpec((FW // 3, D), lambda i: (i, 0)),),
    )(core, w_t, q0, q1, hid)
    (send1,) = call(
        second_pick_kernel, "second_pick", [((SLOTS, 2 * W1), BF)],
        [SMEM, full(3, TOK), full(TOK, D), full(*q1.shape), AFTER],
        [((TOK, 2 * W1), BF)], 200_000_000,
    )(core, pos, out_grad, q1, w_ord)
    recv1 = dispatch(send1)

    def tail(rows, width, after):
        size = rows.shape[1] - width
        (out,) = call(
            tail_kernel, "tail", [((SLOTS, size), BF)],
            [full(*rows.shape), AFTER], (), 1_000_000, 1,
        )(rows, after)
        return lax.ppermute(out, "c", swap)

    peer0 = tail(recv0, W0, send1)
    part0, sh = call(
        first_grad_kernel, "first_grad",
        [((NY, 512, 128), BF), ((2 * SLOTS, FW), BF)],
        [block(SLOTS, W0, 0), block(SLOTS, 128, 2 * W0 // 128), full(SLOTS, W0 + 128),
         full(2 * SLOTS, FW)],
        [((W0, FW), F32)], 400_000_000, 6,
    )(recv0, recv0, peer0, hid)
    got0 = exchange(part0, "y")
    peer1 = tail(recv1, W1, part0)
    third = FW // 3
    pg_t, slot_grad = call(
        pre_kernel, "pre", [((2, FW, SLOTS), BF), ((1, SLOTS), F32)],
        [pl.BlockSpec((third, D), lambda i: (i, 0)), full(SLOTS, 2 * W0 + 128), full(SLOTS, 2 * W1),
         pl.BlockSpec((third, SLOTS), lambda i: (i, 0)),
         pl.BlockSpec((third, SLOTS), lambda i: (3 + i, 0))],
        (), 700_000_000, 9, 63, 3,
        (pl.BlockSpec((2, third, SLOTS), lambda i: (0, i, 0)), full(1, SLOTS)),
    )(w_ord, recv0, recv1, sp_t, sp_t)
    (part1,) = call(
        second_grad_kernel, "second_grad", [((NY, 336, 128), BF)],
        [block(SLOTS, W1, 0), full(SLOTS, W1), full(2 * SLOTS, FW), AFTER],
        [((W1, FW), F32)], 270_000_000, 4,
    )(recv1, peer1, sh, slot_grad)
    def ring(n, by):
        return [(i, (i + by) % n) for i in range(n)]

    row = slot_grad
    for by in (1, 2):
        row = jnp.concatenate([row, lax.ppermute(row, "x", ring(NX, by))], axis=0)
    part1 = pl.pallas_call(
        gate_kernel,
        out_shape=jax.ShapeDtypeStruct(part1.shape, part1.dtype),
        in_specs=[AFTER, AFTER, AFTER],
        out_specs=AFTER,
        input_output_aliases={0: 0},
        compiler_params=pltpu.CompilerParams(vmem_limit_bytes=63 * 1024 * 1024),
        name="gate",
    )(part1, got0, row)
    got1 = exchange(part1, "y")
    every = jnp.concatenate(
        [row] + [lax.ppermute(row, "zl", ring(NZL, d)) for d in range(1, NZL)], axis=0
    )
    (prob_t,) = call(
        back_kernel, "back", [((3, TOK), F32)],
        [SMEM, SMEM, full(3, TOK), full(3, TOK), full(12, SLOTS)], (), 1_000_000, 1,
    )(scalar("zl"), scalar("x"), picks.T, pos, every)
    (sums,) = call(
        sum_kernel, "sum", [((NZ * OWN, FW), BF)],
        [full(NY, 512, 128), full(NY, 336, 128), AFTER], (), 1_000_000, 2, 16,
    )(got0, got1, prob_t)
    over_z = exchange(sums.reshape(NZ, OWN, FW), "z")
    (down_grad,) = call(
        last_kernel, "last", [((OWN, FW), F32)], [full(NZ, OWN, FW)], (), 1_000_000, 1, 16,
    )(over_z)
    return (pg_t.reshape(2 * FW, SLOTS).T, down_grad[None], prob_t.T)


def solution(mesh):
    names = ("y", "z", "c", "zl", "x")
    cut = Mesh(mesh.devices.reshape(NY, NZ, NC, NZL, NX), names)
    rows = P(names, None)
    in_specs = (rows, rows, rows, rows, P(("zl", "x"), None, None))
    out_specs = (rows, P(("zl", "x"), ("y", "z", "c"), None), rows)
    return jax.shard_map(
        on_device, mesh=cut, in_specs=in_specs, out_specs=out_specs, check_vma=False
    )
```

```python
import jax
import jax.numpy as jnp
import numpy as np
from jax import lax
from jax.experimental import pallas as pl
from jax.experimental.pallas import tpu as pltpu
from jax.sharding import Mesh, PartitionSpec as P

BF = jnp.bfloat16
F32 = jnp.float32
NY, NZ, NC, NZL, NX = 8, 4, 2, 3, 4
D, FW, TOK, SLOTS, OWN = 2560, 672, 128, 384, 40
BLK = D // 4
HALF = D // 2
R = HALF // NY
PACKED = 848
ROWS_T = (((0,), (0,)), ((), ()))
LANES_T = (((1,), (1,)), ((), ()))


def split_matrix():
    n = np.arange(BLK)
    h, yz, i = n // 320, n % 320 // OWN, n % OWN
    m = np.zeros((BLK, BLK), np.float32)
    m[yz * 80 + h * OWN + i, n] = 1.0
    return jnp.asarray(m, BF)


def one_hot(mask):
    return jnp.where(mask, 1.0, 0.0).astype(BF)


def reorder(ref, q_ref, core, out_ref):
    y = [
        jnp.dot(ref[:, BLK * k : BLK * (k + 1)], q_ref[...], preferred_element_type=F32)
        for k in range(4)
    ]
    for h in range(2):
        at = pl.multiple_of((core ^ h) * HALF, 128)
        out_ref[:, pl.ds(at, HALF)] = jnp.concatenate(
            [v[:, 320 * h : 320 * (h + 1)] for v in y], axis=1
        ).astype(BF)


def pick_kernel(core_ref, picks_ref, probs_ref, og_ref, q_ref, out_ref, pos_ref, x_ref):
    g = pl.program_id(0)

    @pl.when(g == 0)
    def _():
        reorder(og_ref, q_ref, core_ref[0], x_ref)

    row = lax.broadcasted_iota(jnp.int32, (TOK, TOK), 0)
    col = lax.broadcasted_iota(jnp.int32, (TOK, TOK), 1)
    value = lax.broadcasted_iota(jnp.int32, (16, TOK), 0)
    chosen = picks_ref[pl.ds(g, 1), :] == value
    rank = jnp.dot(one_hot(chosen), one_hot(row < col), preferred_element_type=F32)
    pos = jnp.sum(jnp.where(chosen, rank + 32.0 * value.astype(F32), 0.0), axis=0, keepdims=True)
    pos = pos.astype(jnp.int32)
    pos_ref[pl.ds(g, 1), :] = pos
    sel = row == pos
    out_ref[:, :D] = jnp.dot(one_hot(sel), x_ref[...], preferred_element_type=F32).astype(BF)
    group = lax.broadcasted_iota(jnp.int32, (3, TOK), 0) == g
    prob = jnp.sum(jnp.where(group, probs_ref[...].astype(F32), 0.0), axis=0, keepdims=True)
    pr = jnp.sum(jnp.where(sel, prob, 0.0), axis=1, keepdims=True)
    out_ref[:, D:] = jnp.broadcast_to(pr, (TOK, 128)).astype(BF)


def hidden_kernel(own_ref, peer_ref, after_ref, out_ref):
    for k, ref in enumerate((own_ref, peer_ref)):
        gate = ref[:FW, :].astype(F32)
        up = ref[FW:, :].astype(F32)
        out_ref[k * SLOTS : (k + 1) * SLOTS, :] = (gate * jax.nn.sigmoid(gate) * up).T


def gate_kernel(x_ref, after_ref, out_ref):
    pass


def order_kernel(core_ref, w_ref, q_ref, after_ref, out_ref):
    reorder(w_ref, q_ref, core_ref[0], out_ref)


def grad_kernel(own_ref, prob_ref, peer_ref, peer_prob_ref, hid_ref, out_ref, sh_ref, acc_ref):
    @pl.when(pl.program_id(0) == 0)
    def _():
        for k, ref in enumerate((prob_ref, peer_prob_ref)):
            p = ref[...].astype(F32)
            for a in range(0, FW, 128):
                b = min(a + 128, FW)
                sh_ref[k * SLOTS : (k + 1) * SLOTS, a:b] = (
                    p[:, : b - a] * hid_ref[k * SLOTS : (k + 1) * SLOTS, a:b]
                ).astype(BF)

    for a in range(0, acc_ref.shape[0], 128):
        acc_ref[a : a + 128, :] = lax.dot_general(
            own_ref[:, a : a + 128], sh_ref[:SLOTS, :], ROWS_T, preferred_element_type=F32
        ) + lax.dot_general(
            peer_ref[:, a : a + 128], sh_ref[SLOTS:, :], ROWS_T, preferred_element_type=F32
        )
    quarter = R // 4
    for y in range(out_ref.shape[0]):
        for j in range(5):
            out_ref[y, R * j : R * (j + 1), :] = acc_ref[
                R * y : R * (y + 1), 128 * j : 128 * (j + 1)
            ].astype(BF)
        last = jnp.concatenate(
            [acc_ref[R * y + quarter * n : R * y + quarter * (n + 1), 640:] for n in range(4)],
            axis=1,
        )
        fill = jnp.zeros((PACKED - 5 * R - quarter, 128), F32)
        out_ref[y, 5 * R :, :] = jnp.concatenate([last, fill], axis=0).astype(BF)


def sum_kernel(x_ref, after_ref, out_ref):
    total = x_ref[0].astype(F32)
    for n in range(1, NY):
        total += x_ref[n].astype(F32)
    last = total[5 * R : 5 * R + R // 4]
    out_ref[...] = jnp.concatenate(
        [total[R * j : R * (j + 1)] for j in range(5)]
        + [jnp.concatenate([last[:, 32 * n : 32 * (n + 1)] for n in range(4)], axis=0)],
        axis=1,
    ).astype(BF)


def last_kernel(x_ref, out_ref):
    total = x_ref[0].astype(F32)
    for n in range(1, NZ):
        total += x_ref[n].astype(F32)
    out_ref[...] = total


def pre_kernel(w_ref, rows_ref, gate_ref, up_ref, after_ref, pg_ref, sg_ref):
    lane = lax.broadcasted_iota(jnp.int32, (16, 128), 1)
    prob = lax.dot_general(
        one_hot(lane == 0), rows_ref[:, D:], LANES_T, preferred_element_type=F32
    )[:1]
    proj = lax.dot_general(w_ref[...], rows_ref[:, :D], LANES_T, preferred_element_type=F32)
    gate = gate_ref[...].astype(F32)
    up = up_ref[...].astype(F32)
    sig = jax.nn.sigmoid(gate)
    act = gate * sig
    part = jnp.sum(act * up * proj, axis=0, keepdims=True)
    sg_ref[...] = jnp.where(pl.program_id(0) == 0, part, part + sg_ref[...])
    hg = prob * proj
    pg_ref[0] = (hg * up * sig * (1.0 + gate * (1.0 - sig))).astype(BF)
    pg_ref[1] = (hg * act).astype(BF)


def back_kernel(zl_ref, x_ref, picks_ref, pos_ref, every_ref, out_ref):
    zl, x = zl_ref[0], x_ref[0]
    lane = lax.broadcasted_iota(jnp.int32, (SLOTS, TOK), 0)
    row = lax.broadcasted_iota(jnp.int32, (12, TOK), 0)
    for g in range(3):
        pick = picks_ref[g : g + 1, :]
        rank = pos_ref[g : g + 1, :] - 32 * pick
        at = jnp.where(lane == rank + 32 * (NX * zl + x), 1.0, 0.0)
        got = jnp.dot(
            every_ref[...], at, preferred_element_type=F32, precision=lax.Precision.HIGHEST
        )
        back = jnp.where(zl >= g, zl - g, zl - g + NZL)
        from_row = NX * back + ((x - pick + NX) & (NX - 1))
        out_ref[g : g + 1, :] = jnp.sum(jnp.where(row == from_row, got, 0.0), axis=0, keepdims=True)


SMEM = pl.BlockSpec(memory_space=pltpu.SMEM)
AFTER = pl.BlockSpec(memory_space=pl.ANY)


def full(*shape):
    return pl.BlockSpec(shape, lambda i: (0,) * len(shape))


def block(rows, columns, at):
    return pl.BlockSpec((rows, columns), lambda i: (0, at))


def call(kernel, name, outs, in_specs, scratch=(), macs=0, mbytes=4, mib=63, steps=1, out_specs=None):
    shapes = tuple(jax.ShapeDtypeStruct(s, t) for s, t in outs)
    return pl.pallas_call(
        kernel,
        grid=(steps,),
        out_shape=shapes,
        in_specs=in_specs,
        out_specs=out_specs or tuple(full(*s) for s, _ in outs),
        scratch_shapes=[pltpu.VMEM(s, t) for s, t in scratch],
        compiler_params=pltpu.CompilerParams(vmem_limit_bytes=mib * 1024 * 1024),
        cost_estimate=pl.CostEstimate(
            flops=2 * macs, bytes_accessed=mbytes * 1_000_000, transcendentals=0
        ),
        name=name,
    )


def gate(x, after):
    return pl.pallas_call(
        gate_kernel,
        out_shape=jax.ShapeDtypeStruct(x.shape, x.dtype),
        in_specs=[AFTER, AFTER],
        out_specs=AFTER,
        input_output_aliases={0: 0},
        compiler_params=pltpu.CompilerParams(vmem_limit_bytes=63 * 1024 * 1024),
        name="gate",
    )(x, after)


def on_device(out_grad, probs, picks, saved_pre, down_weight):
    def scalar(name):
        return lax.axis_index(name).astype(jnp.int32).reshape(1)

    def exchange(blocks, axes):
        return lax.all_to_all(blocks, axes, split_axis=0, concat_axis=0, tiled=True)

    def ring(n, by):
        return [(i, (i + by) % n) for i in range(n)]

    core = scalar("c")
    q = split_matrix()
    sp_t = saved_pre.T
    w_t = down_weight[0].T
    third = FW // 3

    send, pos = call(
        pick_kernel, "pick",
        [((SLOTS, D + 128), BF), ((3, TOK), jnp.int32)],
        [SMEM, full(3, TOK), full(3, TOK), full(TOK, D), full(BLK, BLK)],
        [((TOK, D), BF)], 400_000_000, 4, 63, 3,
        (pl.BlockSpec((TOK, D + 128), lambda i: (i, 0)), full(3, TOK)),
    )(core, picks.T, probs.T, out_grad, q)
    recv = exchange(send.reshape(12, 32, D + 128), ("zl", "x")).reshape(SLOTS, D + 128)
    (hid,) = call(
        hidden_kernel, "hidden", [((2 * SLOTS, FW), F32)],
        [full(2 * FW, SLOTS), full(2 * FW, SLOTS), AFTER], (), 500_000_000,
    )(sp_t, lax.ppermute(sp_t, "c", ring(2, 1)), pos)
    (w_ord,) = call(
        order_kernel, "order", [((FW, D), BF)],
        [SMEM, pl.BlockSpec((third, D), lambda i: (i, 0)), full(BLK, BLK), AFTER],
        (), 1_000_000_000, 10, 63, 3, (pl.BlockSpec((third, D), lambda i: (i, 0)),),
    )(core, w_t, q, hid)

    recv = gate(recv, w_ord)
    peer = lax.ppermute(recv[:, HALF:], "c", ring(2, 1))
    (part,) = call(
        grad_kernel, "grad", [((NY, PACKED, 128), BF)],
        [pl.BlockSpec((SLOTS, BLK), lambda i: (0, i)), block(SLOTS, 128, D // 128),
         pl.BlockSpec((SLOTS, BLK), lambda i: (0, i)), block(SLOTS, 128, HALF // 128),
         full(2 * SLOTS, FW)],
        [((2 * SLOTS, FW), BF), ((BLK, FW), F32)], 700_000_000, 7, 63, 2,
        (pl.BlockSpec((NY // 2, PACKED, 128), lambda i: (i, 0, 0)),),
    )(recv, recv, peer, peer, hid)
    over_y = exchange(part, "y")

    pg_t, slot_grad = call(
        pre_kernel, "pre", [((2, FW, SLOTS), BF), ((1, SLOTS), F32)],
        [pl.BlockSpec((third, D), lambda i: (i, 0)), full(SLOTS, D + 128),
         pl.BlockSpec((third, SLOTS), lambda i: (i, 0)),
         pl.BlockSpec((third, SLOTS), lambda i: (3 + i, 0)), AFTER],
        (), 700_000_000, 9, 63, 3,
        (pl.BlockSpec((2, third, SLOTS), lambda i: (0, i, 0)), full(1, SLOTS)),
    )(w_ord, recv, sp_t, sp_t, part)
    row = slot_grad
    for by in (1, 2):
        row = jnp.concatenate([row, lax.ppermute(row, "x", ring(NX, by))], axis=0)
    every = jnp.concatenate(
        [row] + [lax.ppermute(row, "zl", ring(NZL, d)) for d in range(1, NZL)], axis=0
    )
    (prob_t,) = call(
        back_kernel, "back", [((3, TOK), F32)],
        [SMEM, SMEM, full(3, TOK), full(3, TOK), full(12, SLOTS)], (), 1_000_000, 1,
    )(scalar("zl"), scalar("x"), picks.T, pos, every)
    (sums,) = call(
        sum_kernel, "sum", [((NZ * OWN, FW), BF)],
        [full(NY, PACKED, 128), AFTER], (), 1_000_000, 2, 16,
    )(over_y, prob_t)
    over_z = exchange(sums.reshape(NZ, OWN, FW), "z")
    (down_grad,) = call(
        last_kernel, "last", [((OWN, FW), F32)], [full(NZ, OWN, FW)], (), 1_000_000, 1, 16,
    )(over_z)
    return (pg_t.reshape(2 * FW, SLOTS).T, down_grad[None], prob_t.T)


def solution(mesh):
    names = ("y", "z", "c", "zl", "x")
    cut = Mesh(mesh.devices.reshape(NY, NZ, NC, NZL, NX), names)
    rows = P(names, None)
    in_specs = (rows, rows, rows, rows, P(("zl", "x"), None, None))
    out_specs = (rows, P(("zl", "x"), ("y", "z", "c"), None), rows)
    return jax.shard_map(
        on_device, mesh=cut, in_specs=in_specs, out_specs=out_specs, check_vma=False
    )
```

```python
import jax
import jax.numpy as jnp
import numpy as np
from jax import lax
from jax.experimental import pallas as pl
from jax.experimental.pallas import tpu as pltpu
from jax.sharding import Mesh, PartitionSpec as P

BF = jnp.bfloat16
F32 = jnp.float32
NK, NP, NY, NZ, NC, NZL, NX = 4, 2, 8, 4, 2, 3, 4
D, FW, TOK, SLOTS, OWN = 2560, 672, 128, 384, 40
BLK = D // 4
FIRST = 24
W0, W1 = D // 2 * FIRST // OWN, D // 2 * (OWN - FIRST) // OWN
R0, R1 = W0 // NY, W1 // NY
ROWS_T = (((0,), (0,)), ((), ()))
LANES_T = (((1,), (1,)), ((), ()))


def split_matrix(start, size):
    n = np.arange(16 * size)
    h, y, z, i = n // (8 * size), n // (4 * size) % 2, n // size % 4, n % size
    m = np.zeros((BLK, 16 * size), np.float32)
    m[y * 320 + z * 80 + h * OWN + start + i, n] = 1.0
    return jnp.asarray(m, BF)


def one_hot(mask):
    return jnp.where(mask, 1.0, 0.0).astype(BF)


def reorder(ref, q_ref, core, out_ref, base):
    part = q_ref.shape[1] // 2
    y = [
        jnp.dot(ref[:, BLK * k : BLK * (k + 1)], q_ref[...], preferred_element_type=F32)
        for k in range(4)
    ]
    for h in range(2):
        at = pl.multiple_of((core ^ h) * 4 * part + base, 128)
        out_ref[:, pl.ds(at, 4 * part)] = jnp.concatenate(
            [v[:, part * h : part * (h + 1)] for v in y], axis=1
        ).astype(BF)


def first_pick_kernel(core_ref, picks_ref, probs_ref, og_ref, q_ref, out_ref, pos_ref, x_ref):
    reorder(og_ref, q_ref, core_ref[0], x_ref, 0)
    row = lax.broadcasted_iota(jnp.int32, (TOK, TOK), 0)
    col = lax.broadcasted_iota(jnp.int32, (TOK, TOK), 1)
    before = one_hot(row < col)
    value = lax.broadcasted_iota(jnp.int32, (16, TOK), 0)
    for g in range(3):
        chosen = picks_ref[g : g + 1, :] == value
        rank = jnp.dot(one_hot(chosen), before, preferred_element_type=F32)
        pos = jnp.sum(jnp.where(chosen, rank + 32.0 * value.astype(F32), 0.0), axis=0, keepdims=True)
        pos = pos.astype(jnp.int32)
        pos_ref[g : g + 1, :] = pos
        sel = row == pos
        out_ref[g * TOK : (g + 1) * TOK, : 2 * W0] = jnp.dot(
            one_hot(sel), x_ref[...], preferred_element_type=F32
        ).astype(BF)
        pr = jnp.sum(
            jnp.where(sel, probs_ref[g : g + 1, :].astype(F32), 0.0), axis=1, keepdims=True
        )
        out_ref[g * TOK : (g + 1) * TOK, 2 * W0 :] = jnp.broadcast_to(pr, (TOK, 128)).astype(BF)


def second_pick_kernel(core_ref, pos_ref, og_ref, q_ref, after_ref, out_ref, x_ref):
    reorder(og_ref, q_ref, core_ref[0], x_ref, 0)
    row = lax.broadcasted_iota(jnp.int32, (TOK, TOK), 0)
    for g in range(3):
        out_ref[g * TOK : (g + 1) * TOK, :] = jnp.dot(
            one_hot(row == pos_ref[g : g + 1, :]), x_ref[...], preferred_element_type=F32
        ).astype(BF)


def hidden_kernel(own_ref, peer_ref, after_ref, out_ref):
    for k, ref in enumerate((own_ref, peer_ref)):
        gate = ref[:FW, :].astype(F32)
        up = ref[FW:, :].astype(F32)
        out_ref[k * SLOTS : (k + 1) * SLOTS, :] = (gate * jax.nn.sigmoid(gate) * up).T


def order_kernel(core_ref, w_ref, q0_ref, q1_ref, after_ref, out_ref):
    reorder(w_ref, q0_ref, core_ref[0], out_ref, 0)
    reorder(w_ref, q1_ref, core_ref[0], out_ref, 2 * W0)


def partial_grad(own_ref, peer_ref, sh_ref, acc_ref):
    for a in range(0, acc_ref.shape[0], 128):
        acc_ref[a : a + 128, :] = lax.dot_general(
            own_ref[:, a : a + 128], sh_ref[:SLOTS, :], ROWS_T, preferred_element_type=F32
        ) + lax.dot_general(
            peer_ref[:, a : a + 128], sh_ref[SLOTS:, :], ROWS_T, preferred_element_type=F32
        )


def pack(block, out_ref, at):
    rows = block.shape[0]
    quarter = rows // 4
    for j in range(5):
        out_ref[at, rows * j : rows * (j + 1), :] = block[:, 128 * j : 128 * (j + 1)].astype(
            out_ref.dtype
        )
    last = jnp.concatenate(
        [block[quarter * n : quarter * (n + 1), 640:] for n in range(4)], axis=1
    )
    fill = out_ref.shape[1] - 5 * rows - quarter
    if fill:
        last = jnp.concatenate([last, jnp.zeros((fill, 128), F32)], axis=0)
    out_ref[at, 5 * rows :, :] = last.astype(out_ref.dtype)


def first_grad_kernel(
    par_ref, own_ref, prob_ref, peer_ref, hid_ref, keep_ref, a_ref, b_ref, sh_ref, acc_ref
):
    for k, p in enumerate((prob_ref[...], peer_ref[:, W0:])):
        p = p.astype(F32)
        for a in range(0, FW, 128):
            b = min(a + 128, FW)
            sh_ref[k * SLOTS : (k + 1) * SLOTS, a:b] = (
                p[:, : b - a] * hid_ref[k * SLOTS : (k + 1) * SLOTS, a:b]
            ).astype(BF)
    partial_grad(own_ref, peer_ref, sh_ref, acc_ref)
    par = par_ref[0]
    for k in range(NK):
        for y, to_ref, at in (
            (2 * k + par, keep_ref, k),
            (2 * k + 1 - par, (a_ref, b_ref)[k // 2], k % 2),
        ):
            pack(acc_ref[pl.ds(pl.multiple_of(R0 * y, 32), R0), :], to_ref, at)


def second_grad_kernel(own_ref, peer_ref, sh_ref, out_ref, acc_ref):
    partial_grad(own_ref, peer_ref, sh_ref, acc_ref)
    for y in range(NY):
        pack(acc_ref[R1 * y : R1 * (y + 1), :], out_ref, y)


def pair_kernel(keep_ref, a_ref, b_ref, out_ref):
    out_ref[:2] = (keep_ref[:2] + a_ref[...].astype(F32)).astype(BF)
    out_ref[2:] = (keep_ref[2:] + b_ref[...].astype(F32)).astype(BF)


def gate_kernel(x_ref, after_ref, out_ref):
    pass


def unpacked_sum(ref, rows):
    total = ref[0].astype(F32)
    for n in range(1, ref.shape[0]):
        total += ref[n].astype(F32)
    last = total[5 * rows : 5 * rows + rows // 4]
    return jnp.concatenate(
        [total[rows * j : rows * (j + 1)] for j in range(5)]
        + [jnp.concatenate([last[:, 32 * n : 32 * (n + 1)] for n in range(4)], axis=0)],
        axis=1,
    )


def sum_kernel(x0_ref, x1_ref, after_ref, out_ref):
    x0, x1 = unpacked_sum(x0_ref, R0), unpacked_sum(x1_ref, R1)
    out_ref[...] = jnp.concatenate(
        [part[n * z : n * (z + 1)] for z in range(NZ) for part, n in ((x0, R0 // NZ), (x1, R1 // NZ))],
        axis=0,
    ).astype(BF)


def last_kernel(x_ref, out_ref):
    total = x_ref[0].astype(F32)
    for n in range(1, NZ):
        total += x_ref[n].astype(F32)
    out_ref[...] = total


def pre_kernel(w_ref, r0_ref, r1_ref, gate_ref, up_ref, after_ref, pg_ref, sg_ref):
    lane = lax.broadcasted_iota(jnp.int32, (16, 128), 1)
    prob = lax.dot_general(
        one_hot(lane == 0), r0_ref[:, 2 * W0 :], LANES_T, preferred_element_type=F32
    )[:1]
    proj = lax.dot_general(
        w_ref[:, : 2 * W0], r0_ref[:, : 2 * W0], LANES_T, preferred_element_type=F32
    ) + lax.dot_general(w_ref[:, 2 * W0 :], r1_ref[...], LANES_T, preferred_element_type=F32)
    gate = gate_ref[...].astype(F32)
    up = up_ref[...].astype(F32)
    sig = jax.nn.sigmoid(gate)
    act = gate * sig
    part = jnp.sum(act * up * proj, axis=0, keepdims=True)
    sg_ref[...] = jnp.where(pl.program_id(0) == 0, part, part + sg_ref[...])
    hg = prob * proj
    pg_ref[0] = (hg * up * sig * (1.0 + gate * (1.0 - sig))).astype(BF)
    pg_ref[1] = (hg * act).astype(BF)


def back_kernel(here_ref, picks_ref, pos_ref, every_ref, out_ref):
    lane = lax.broadcasted_iota(jnp.int32, (SLOTS, TOK), 0)
    row = lax.broadcasted_iota(jnp.int32, (12, TOK), 0)
    for g in range(3):
        pick = picks_ref[g : g + 1, :]
        rank = pos_ref[g : g + 1, :] - 32 * pick
        at = jnp.where(lane == rank + 32 * here_ref[0], 1.0, 0.0)
        got = jnp.dot(
            every_ref[...], at, preferred_element_type=F32, precision=lax.Precision.HIGHEST
        )
        out_ref[g : g + 1, :] = jnp.sum(
            jnp.where(row == NX * g + pick, got, 0.0), axis=0, keepdims=True
        )


SMEM = pl.BlockSpec(memory_space=pltpu.SMEM)
AFTER = pl.BlockSpec(memory_space=pl.ANY)


def full(*shape):
    return pl.BlockSpec(shape, lambda i: (0,) * len(shape))


def block(rows, columns, at):
    return pl.BlockSpec((rows, columns), lambda i: (0, at))


def call(kernel, name, outs, in_specs, scratch=(), macs=0, mbytes=4, mib=63, steps=1, out_specs=None):
    shapes = tuple(jax.ShapeDtypeStruct(s, t) for s, t in outs)
    return pl.pallas_call(
        kernel,
        grid=(steps,),
        out_shape=shapes,
        in_specs=in_specs,
        out_specs=out_specs or tuple(full(*s) for s, _ in outs),
        scratch_shapes=[pltpu.VMEM(s, t) for s, t in scratch],
        compiler_params=pltpu.CompilerParams(vmem_limit_bytes=mib * 1024 * 1024),
        cost_estimate=pl.CostEstimate(
            flops=2 * macs, bytes_accessed=mbytes * 1_000_000, transcendentals=0
        ),
        name=name,
    )


def gate(x, after):
    return pl.pallas_call(
        gate_kernel,
        out_shape=jax.ShapeDtypeStruct(x.shape, x.dtype),
        in_specs=[AFTER, AFTER],
        out_specs=AFTER,
        input_output_aliases={0: 0},
        compiler_params=pltpu.CompilerParams(vmem_limit_bytes=63 * 1024 * 1024),
        name="gate",
    )(x, after)


def on_device(out_grad, probs, picks, saved_pre, down_weight):
    def scalar(name):
        return lax.axis_index(name).astype(jnp.int32).reshape(1)

    core = scalar("c")
    swap = [(0, 1), (1, 0)]
    q0, q1 = split_matrix(0, FIRST), split_matrix(FIRST, OWN - FIRST)
    sp_t = saved_pre.T
    w_t = down_weight[0].T

    def exchange(blocks, axes):
        return lax.all_to_all(blocks, axes, split_axis=0, concat_axis=0, tiled=True)

    def dispatch(rows):
        return exchange(rows.reshape(12, 32, -1), ("zl", "x")).reshape(SLOTS, -1)

    send0, pos = call(
        first_pick_kernel, "first_pick",
        [((SLOTS, 2 * W0 + 128), BF), ((3, TOK), jnp.int32)],
        [SMEM, full(3, TOK), full(3, TOK), full(TOK, D), full(*q0.shape)],
        [((TOK, 2 * W0), BF)], 200_000_000,
    )(core, picks.T, probs.T, out_grad, q0)
    recv0 = dispatch(send0)
    (hid,) = call(
        hidden_kernel, "hidden", [((2 * SLOTS, FW), F32)],
        [full(2 * FW, SLOTS), full(2 * FW, SLOTS), AFTER], (), 500_000_000,
    )(sp_t, lax.ppermute(sp_t, "c", swap), pos)
    (w_ord,) = call(
        order_kernel, "order", [((FW, D), BF)],
        [SMEM, pl.BlockSpec((FW // 3, D), lambda i: (i, 0)), full(*q0.shape), full(*q1.shape), AFTER],
        (), 1_000_000_000, 10, 63, 3, (pl.BlockSpec((FW // 3, D), lambda i: (i, 0)),),
    )(core, w_t, q0, q1, hid)
    (send1,) = call(
        second_pick_kernel, "second_pick", [((SLOTS, 2 * W1), BF)],
        [SMEM, full(3, TOK), full(TOK, D), full(*q1.shape), AFTER],
        [((TOK, 2 * W1), BF)], 200_000_000,
    )(core, pos, out_grad, q1, w_ord)
    recv1 = dispatch(send1)

    up_pair = [(y, y ^ 1) for y in range(NY)]
    down_pair = [(y, (y + 1 if y % 2 else y - 1) % NY) for y in range(NY)]
    third = FW // 3

    recv0 = gate(recv0, send1)
    peer0 = lax.ppermute(recv0[:, W0:], "c", swap)
    keep0, a0, b0, sh = call(
        first_grad_kernel, "first_grad",
        [((NK, 512, 128), F32), ((2, 512, 128), BF), ((2, 512, 128), BF), ((2 * SLOTS, FW), BF)],
        [SMEM, block(SLOTS, W0, 0), block(SLOTS, 128, 2 * W0 // 128), full(SLOTS, W0 + 128),
         full(2 * SLOTS, FW)],
        [((W0, FW), F32)], 400_000_000, 6,
    )(scalar("p"), recv0, recv0, peer0, hid)
    a0 = lax.ppermute(a0, ("k", "p"), up_pair)
    b0 = lax.ppermute(b0, ("k", "p"), down_pair)
    recv1 = gate(recv1, keep0)
    (half0,) = call(
        pair_kernel, "pair", [((NK, 512, 128), BF)],
        [full(NK, 512, 128), full(2, 512, 128), full(2, 512, 128)], (), 1_000_000, 2, 16,
    )(keep0, a0, b0)
    got0 = exchange(half0, "k")
    peer1 = lax.ppermute(recv1[:, W1:], "c", swap)
    (part1,) = call(
        second_grad_kernel, "second_grad", [((NY, 336, 128), BF)],
        [block(SLOTS, W1, 0), full(SLOTS, W1), full(2 * SLOTS, FW)],
        [((W1, FW), F32)], 270_000_000, 4,
    )(recv1, peer1, sh)
    part1 = gate(part1, got0)
    got1 = exchange(part1, ("k", "p"))
    pg_t, slot_grad = call(
        pre_kernel, "pre", [((2, FW, SLOTS), BF), ((1, SLOTS), F32)],
        [pl.BlockSpec((third, D), lambda i: (i, 0)), full(SLOTS, 2 * W0 + 128), full(SLOTS, 2 * W1),
         pl.BlockSpec((third, SLOTS), lambda i: (i, 0)),
         pl.BlockSpec((third, SLOTS), lambda i: (3 + i, 0)), AFTER],
        (), 700_000_000, 9, 63, 3,
        (pl.BlockSpec((2, third, SLOTS), lambda i: (0, i, 0)), full(1, SLOTS)),
    )(w_ord, recv0, recv1, sp_t, sp_t, part1)
    row = lax.all_gather(slot_grad, "x", axis=0, tiled=True)
    every = lax.all_gather(row, "zl", axis=0, tiled=True)
    (prob_t,) = call(
        back_kernel, "back", [((3, TOK), F32)],
        [SMEM, full(3, TOK), full(3, TOK), full(12, SLOTS)], (), 1_000_000, 1,
    )(scalar("zl") * NX + scalar("x"), picks.T, pos, every)
    (sums,) = call(
        sum_kernel, "sum", [((NZ * OWN, FW), BF)],
        [full(NK, 512, 128), full(NY, 336, 128), AFTER], (), 1_000_000, 2, 16,
    )(got0, got1, prob_t)
    over_z = exchange(sums.reshape(NZ, OWN, FW), "z")
    (down_grad,) = call(
        last_kernel, "last", [((OWN, FW), F32)], [full(NZ, OWN, FW)], (), 1_000_000, 1, 16,
    )(over_z)
    return (pg_t.reshape(2 * FW, SLOTS).T, down_grad[None], prob_t.T)


def solution(mesh):
    names = ("k", "p", "z", "c", "zl", "x")
    cut = Mesh(mesh.devices.reshape(NK, NP, NZ, NC, NZL, NX), names)
    rows = P(names, None)
    in_specs = (rows, rows, rows, rows, P(("zl", "x"), None, None))
    out_specs = (rows, P(("zl", "x"), ("k", "p", "z", "c"), None), rows)
    return jax.shard_map(
        on_device, mesh=cut, in_specs=in_specs, out_specs=out_specs, check_vma=False
    )
```

```python
import jax
import jax.numpy as jnp
import numpy as np
from jax import lax
from jax.experimental import pallas as pl
from jax.experimental.pallas import tpu as pltpu
from jax.sharding import Mesh, PartitionSpec as P

BF = jnp.bfloat16
F32 = jnp.float32
NY, NZ, NC, NZL, NX = 8, 4, 2, 3, 4
D, FW, TOK, SLOTS, OWN = 2560, 672, 128, 384, 40
BLK = D // 4
HALF = D // 2
PARTS = NY * NZ
PACKED = 216
ROWS_T = (((0,), (0,)), ((), ()))
LANES_T = (((1,), (1,)), ((), ()))


def split_matrix():
    n = np.arange(BLK)
    h, yz, i = n // 320, n % 320 // OWN, n % OWN
    m = np.zeros((BLK, BLK), np.float32)
    m[yz * 80 + h * OWN + i, n] = 1.0
    return jnp.asarray(m, BF)


def one_hot(mask):
    return jnp.where(mask, 1.0, 0.0).astype(BF)


def reorder(ref, q_ref, core, out_ref):
    y = [
        jnp.dot(ref[:, BLK * k : BLK * (k + 1)], q_ref[...], preferred_element_type=F32)
        for k in range(4)
    ]
    for h in range(2):
        at = pl.multiple_of((core ^ h) * HALF, 128)
        out_ref[:, pl.ds(at, HALF)] = jnp.concatenate(
            [v[:, 320 * h : 320 * (h + 1)] for v in y], axis=1
        ).astype(BF)


def pick_kernel(core_ref, picks_ref, probs_ref, og_ref, q_ref, out_ref, pos_ref, x_ref):
    g = pl.program_id(0)

    @pl.when(g == 0)
    def _():
        reorder(og_ref, q_ref, core_ref[0], x_ref)

    row = lax.broadcasted_iota(jnp.int32, (TOK, TOK), 0)
    col = lax.broadcasted_iota(jnp.int32, (TOK, TOK), 1)
    value = lax.broadcasted_iota(jnp.int32, (16, TOK), 0)
    chosen = picks_ref[pl.ds(g, 1), :] == value
    rank = jnp.dot(one_hot(chosen), one_hot(row < col), preferred_element_type=F32)
    pos = jnp.sum(jnp.where(chosen, rank + 32.0 * value.astype(F32), 0.0), axis=0, keepdims=True)
    pos = pos.astype(jnp.int32)
    pos_ref[pl.ds(g, 1), :] = pos
    sel = row == pos
    out_ref[:, :D] = jnp.dot(one_hot(sel), x_ref[...], preferred_element_type=F32).astype(BF)
    group = lax.broadcasted_iota(jnp.int32, (3, TOK), 0) == g
    prob = jnp.sum(jnp.where(group, probs_ref[...].astype(F32), 0.0), axis=0, keepdims=True)
    pr = jnp.sum(jnp.where(sel, prob, 0.0), axis=1, keepdims=True)
    out_ref[:, D:] = jnp.broadcast_to(pr, (TOK, 128)).astype(BF)


def hidden_kernel(own_ref, peer_ref, after_ref, out_ref):
    for k, ref in enumerate((own_ref, peer_ref)):
        gate = ref[:FW, :].astype(F32)
        up = ref[FW:, :].astype(F32)
        out_ref[k * SLOTS : (k + 1) * SLOTS, :] = (gate * jax.nn.sigmoid(gate) * up).T


def gate_kernel(x_ref, after_ref, out_ref):
    pass


def order_kernel(core_ref, w_ref, q_ref, after_ref, out_ref):
    reorder(w_ref, q_ref, core_ref[0], out_ref)


def grad_kernel(own_ref, prob_ref, peer_ref, peer_prob_ref, hid_ref, out_ref, sh_ref, acc_ref):
    @pl.when(pl.program_id(0) == 0)
    def _():
        for k, ref in enumerate((prob_ref, peer_prob_ref)):
            p = ref[...].astype(F32)
            for a in range(0, FW, 128):
                b = min(a + 128, FW)
                sh_ref[k * SLOTS : (k + 1) * SLOTS, a:b] = (
                    p[:, : b - a] * hid_ref[k * SLOTS : (k + 1) * SLOTS, a:b]
                ).astype(BF)

    for a in range(0, acc_ref.shape[0], 128):
        acc_ref[a : a + 128, :] = lax.dot_general(
            own_ref[:, a : a + 128], sh_ref[:SLOTS, :], ROWS_T, preferred_element_type=F32
        ) + lax.dot_general(
            peer_ref[:, a : a + 128], sh_ref[SLOTS:, :], ROWS_T, preferred_element_type=F32
        )
    for n in range(out_ref.shape[0]):
        part = acc_ref[OWN * n : OWN * (n + 1), :]
        end = part[:, 640:]
        last = jnp.concatenate([end[32:], jnp.zeros((8, 32), F32)], axis=0)
        last = jnp.concatenate([end[:16], end[16:32], last, jnp.zeros((16, 32), F32)], axis=1)
        out_ref[n] = jnp.concatenate(
            [part[:, 128 * j : 128 * (j + 1)] for j in range(5)] + [last], axis=0
        ).astype(BF)


def sum_kernel(x_ref, out_ref):
    total = x_ref[0].astype(F32)
    for n in range(1, PARTS):
        total += x_ref[n].astype(F32)
    last = total[5 * OWN :]
    last = jnp.concatenate([last[:, :32], last[:, 32:64], last[:8, 64:96]], axis=0)
    out_ref[...] = jnp.concatenate(
        [total[OWN * j : OWN * (j + 1)] for j in range(5)] + [last], axis=1
    )


def pre_kernel(w_ref, rows_ref, gate_ref, up_ref, after_ref, pg_ref, sg_ref):
    lane = lax.broadcasted_iota(jnp.int32, (16, 128), 1)
    prob = lax.dot_general(
        one_hot(lane == 0), rows_ref[:, D:], LANES_T, preferred_element_type=F32
    )[:1]
    proj = lax.dot_general(w_ref[...], rows_ref[:, :D], LANES_T, preferred_element_type=F32)
    gate = gate_ref[...].astype(F32)
    up = up_ref[...].astype(F32)
    sig = jax.nn.sigmoid(gate)
    act = gate * sig
    part = jnp.sum(act * up * proj, axis=0, keepdims=True)
    sg_ref[...] = jnp.where(pl.program_id(0) == 0, part, part + sg_ref[...])
    hg = prob * proj
    pg_ref[0] = (hg * up * sig * (1.0 + gate * (1.0 - sig))).astype(BF)
    pg_ref[1] = (hg * act).astype(BF)


def back_kernel(zl_ref, x_ref, picks_ref, pos_ref, every_ref, out_ref):
    zl, x = zl_ref[0], x_ref[0]
    lane = lax.broadcasted_iota(jnp.int32, (SLOTS, TOK), 0)
    row = lax.broadcasted_iota(jnp.int32, (12, TOK), 0)
    for g in range(3):
        pick = picks_ref[g : g + 1, :]
        rank = pos_ref[g : g + 1, :] - 32 * pick
        at = jnp.where(lane == rank + 32 * (NX * zl + x), 1.0, 0.0)
        got = jnp.dot(
            every_ref[...], at, preferred_element_type=F32, precision=lax.Precision.HIGHEST
        )
        back = jnp.where(zl >= g, zl - g, zl - g + NZL)
        from_row = NX * back + ((x - pick + NX) & (NX - 1))
        out_ref[g : g + 1, :] = jnp.sum(jnp.where(row == from_row, got, 0.0), axis=0, keepdims=True)


SMEM = pl.BlockSpec(memory_space=pltpu.SMEM)
AFTER = pl.BlockSpec(memory_space=pl.ANY)


def full(*shape):
    return pl.BlockSpec(shape, lambda i: (0,) * len(shape))


def block(rows, columns, at):
    return pl.BlockSpec((rows, columns), lambda i: (0, at))


def call(kernel, name, outs, in_specs, scratch=(), macs=0, mbytes=4, mib=63, steps=1, out_specs=None):
    shapes = tuple(jax.ShapeDtypeStruct(s, t) for s, t in outs)
    return pl.pallas_call(
        kernel,
        grid=(steps,),
        out_shape=shapes,
        in_specs=in_specs,
        out_specs=out_specs or tuple(full(*s) for s, _ in outs),
        scratch_shapes=[pltpu.VMEM(s, t) for s, t in scratch],
        compiler_params=pltpu.CompilerParams(vmem_limit_bytes=mib * 1024 * 1024),
        cost_estimate=pl.CostEstimate(
            flops=2 * macs, bytes_accessed=mbytes * 1_000_000, transcendentals=0
        ),
        name=name,
    )


def gate(x, after):
    return pl.pallas_call(
        gate_kernel,
        out_shape=jax.ShapeDtypeStruct(x.shape, x.dtype),
        in_specs=[AFTER, AFTER],
        out_specs=AFTER,
        input_output_aliases={0: 0},
        compiler_params=pltpu.CompilerParams(vmem_limit_bytes=63 * 1024 * 1024),
        name="gate",
    )(x, after)


def on_device(out_grad, probs, picks, saved_pre, down_weight):
    def scalar(name):
        return lax.axis_index(name).astype(jnp.int32).reshape(1)

    def exchange(blocks, axes):
        return lax.all_to_all(blocks, axes, split_axis=0, concat_axis=0, tiled=True)

    def ring(n, by):
        return [(i, (i + by) % n) for i in range(n)]

    core = scalar("c")
    q = split_matrix()
    sp_t = saved_pre.T
    w_t = down_weight[0].T
    third = FW // 3

    send, pos = call(
        pick_kernel, "pick",
        [((SLOTS, D + 128), BF), ((3, TOK), jnp.int32)],
        [SMEM, full(3, TOK), full(3, TOK), full(TOK, D), full(BLK, BLK)],
        [((TOK, D), BF)], 400_000_000, 4, 63, 3,
        (pl.BlockSpec((TOK, D + 128), lambda i: (i, 0)), full(3, TOK)),
    )(core, picks.T, probs.T, out_grad, q)
    recv = exchange(send.reshape(12, 32, D + 128), ("zl", "x")).reshape(SLOTS, D + 128)
    (hid,) = call(
        hidden_kernel, "hidden", [((2 * SLOTS, FW), F32)],
        [full(2 * FW, SLOTS), full(2 * FW, SLOTS), AFTER], (), 500_000_000,
    )(sp_t, lax.ppermute(sp_t, "c", ring(2, 1)), pos)
    (w_ord,) = call(
        order_kernel, "order", [((FW, D), BF)],
        [SMEM, pl.BlockSpec((third, D), lambda i: (i, 0)), full(BLK, BLK), AFTER],
        (), 1_000_000_000, 10, 63, 3, (pl.BlockSpec((third, D), lambda i: (i, 0)),),
    )(core, w_t, q, hid)

    recv = gate(recv, w_ord)
    peer = lax.ppermute(recv[:, HALF:], "c", ring(2, 1))
    (part,) = call(
        grad_kernel, "grad", [((PARTS, PACKED, 128), BF)],
        [pl.BlockSpec((SLOTS, BLK), lambda i: (0, i)), block(SLOTS, 128, D // 128),
         pl.BlockSpec((SLOTS, BLK), lambda i: (0, i)), block(SLOTS, 128, HALF // 128),
         full(2 * SLOTS, FW)],
        [((2 * SLOTS, FW), BF), ((BLK, FW), F32)], 700_000_000, 7, 63, 2,
        (pl.BlockSpec((PARTS // 2, PACKED, 128), lambda i: (i, 0, 0)),),
    )(recv, recv, peer, peer, hid)
    terms = exchange(part, ("y", "z"))

    pg_t, slot_grad = call(
        pre_kernel, "pre", [((2, FW, SLOTS), BF), ((1, SLOTS), F32)],
        [pl.BlockSpec((third, D), lambda i: (i, 0)), full(SLOTS, D + 128),
         pl.BlockSpec((third, SLOTS), lambda i: (i, 0)),
         pl.BlockSpec((third, SLOTS), lambda i: (3 + i, 0)), AFTER],
        (), 700_000_000, 9, 63, 3,
        (pl.BlockSpec((2, third, SLOTS), lambda i: (0, i, 0)), full(1, SLOTS)),
    )(w_ord, recv, sp_t, sp_t, part)
    row = slot_grad
    for by in (1, 2):
        row = jnp.concatenate([row, lax.ppermute(row, "x", ring(NX, by))], axis=0)
    every = jnp.concatenate(
        [row] + [lax.ppermute(row, "zl", ring(NZL, d)) for d in range(1, NZL)], axis=0
    )
    (prob_t,) = call(
        back_kernel, "back", [((3, TOK), F32)],
        [SMEM, SMEM, full(3, TOK), full(3, TOK), full(12, SLOTS)], (), 1_000_000, 1,
    )(scalar("zl"), scalar("x"), picks.T, pos, every)
    (down_grad,) = call(
        sum_kernel, "sum", [((OWN, FW), F32)], [full(PARTS, PACKED, 128)], (), 1_000_000, 2,
    )(gate(terms, prob_t))
    return (pg_t.reshape(2 * FW, SLOTS).T, down_grad[None], prob_t.T)


def solution(mesh):
    names = ("y", "z", "c", "zl", "x")
    cut = Mesh(mesh.devices.reshape(NY, NZ, NC, NZL, NX), names)
    rows = P(names, None)
    in_specs = (rows, rows, rows, rows, P(("zl", "x"), None, None))
    out_specs = (rows, P(("zl", "x"), ("y", "z", "c"), None), rows)
    return jax.shard_map(
        on_device, mesh=cut, in_specs=in_specs, out_specs=out_specs, check_vma=False
    )
```

```python
import jax
import jax.numpy as jnp
import numpy as np
from jax import lax
from jax.experimental import pallas as pl
from jax.experimental.pallas import tpu as pltpu
from jax.sharding import Mesh, PartitionSpec as P

BF = jnp.bfloat16
F32 = jnp.float32
NY, NZ, NC, NZL, NX = 8, 4, 2, 3, 4
D, FW, TOK, SLOTS, OWN = 2560, 672, 128, 384, 40
BLK = D // 4
FIRST = 24
W0, W1 = D // 2 * FIRST // OWN, D // 2 * (OWN - FIRST) // OWN
R0, R1 = W0 // NY, W1 // NY
ROWS_T = (((0,), (0,)), ((), ()))
LANES_T = (((1,), (1,)), ((), ()))


def split_matrix(start, size):
    n = np.arange(16 * size)
    h, y, z, i = n // (8 * size), n // (4 * size) % 2, n // size % 4, n % size
    m = np.zeros((BLK, 16 * size), np.float32)
    m[y * 320 + z * 80 + h * OWN + start + i, n] = 1.0
    return jnp.asarray(m, BF)


def one_hot(mask):
    return jnp.where(mask, 1.0, 0.0).astype(BF)


def reorder(ref, q_ref, core, out_ref, base):
    part = q_ref.shape[1] // 2
    y = [
        jnp.dot(ref[:, BLK * k : BLK * (k + 1)], q_ref[...], preferred_element_type=F32)
        for k in range(4)
    ]
    for h in range(2):
        at = pl.multiple_of((core ^ h) * 4 * part + base, 128)
        out_ref[:, pl.ds(at, 4 * part)] = jnp.concatenate(
            [v[:, part * h : part * (h + 1)] for v in y], axis=1
        ).astype(BF)


def first_pick_kernel(core_ref, picks_ref, probs_ref, og_ref, q_ref, out_ref, pos_ref, x_ref):
    reorder(og_ref, q_ref, core_ref[0], x_ref, 0)
    row = lax.broadcasted_iota(jnp.int32, (TOK, TOK), 0)
    col = lax.broadcasted_iota(jnp.int32, (TOK, TOK), 1)
    before = one_hot(row < col)
    value = lax.broadcasted_iota(jnp.int32, (16, TOK), 0)
    for g in range(3):
        chosen = picks_ref[g : g + 1, :] == value
        rank = jnp.dot(one_hot(chosen), before, preferred_element_type=F32)
        pos = jnp.sum(jnp.where(chosen, rank + 32.0 * value.astype(F32), 0.0), axis=0, keepdims=True)
        pos = pos.astype(jnp.int32)
        pos_ref[g : g + 1, :] = pos
        sel = row == pos
        out_ref[g * TOK : (g + 1) * TOK, : 2 * W0] = jnp.dot(
            one_hot(sel), x_ref[...], preferred_element_type=F32
        ).astype(BF)
        pr = jnp.sum(
            jnp.where(sel, probs_ref[g : g + 1, :].astype(F32), 0.0), axis=1, keepdims=True
        )
        out_ref[g * TOK : (g + 1) * TOK, 2 * W0 :] = jnp.broadcast_to(pr, (TOK, 128)).astype(BF)


def second_pick_kernel(core_ref, pos_ref, og_ref, q_ref, after_ref, out_ref, x_ref):
    reorder(og_ref, q_ref, core_ref[0], x_ref, 0)
    row = lax.broadcasted_iota(jnp.int32, (TOK, TOK), 0)
    for g in range(3):
        out_ref[g * TOK : (g + 1) * TOK, :] = jnp.dot(
            one_hot(row == pos_ref[g : g + 1, :]), x_ref[...], preferred_element_type=F32
        ).astype(BF)


def hidden_kernel(own_ref, peer_ref, after_ref, out_ref):
    for k, ref in enumerate((own_ref, peer_ref)):
        gate = ref[:FW, :].astype(F32)
        up = ref[FW:, :].astype(F32)
        out_ref[k * SLOTS : (k + 1) * SLOTS, :] = (gate * jax.nn.sigmoid(gate) * up).T


def order_kernel(core_ref, w_ref, q0_ref, q1_ref, after_ref, out_ref):
    reorder(w_ref, q0_ref, core_ref[0], out_ref, 0)
    reorder(w_ref, q1_ref, core_ref[0], out_ref, 2 * W0)


def partial_grad(own_ref, peer_ref, sh_ref, out_ref, acc_ref):
    rows = acc_ref.shape[0] // NY
    quarter = rows // 4
    for a in range(0, acc_ref.shape[0], 128):
        acc_ref[a : a + 128, :] = lax.dot_general(
            own_ref[:, a : a + 128], sh_ref[:SLOTS, :], ROWS_T, preferred_element_type=F32
        ) + lax.dot_general(
            peer_ref[:, a : a + 128], sh_ref[SLOTS:, :], ROWS_T, preferred_element_type=F32
        )
    for y in range(NY):
        for j in range(5):
            out_ref[y, rows * j : rows * (j + 1), :] = acc_ref[
                rows * y : rows * (y + 1), 128 * j : 128 * (j + 1)
            ].astype(BF)
        last = jnp.concatenate(
            [
                acc_ref[rows * y + quarter * n : rows * y + quarter * (n + 1), 640:]
                for n in range(4)
            ],
            axis=1,
        )
        fill = out_ref.shape[1] - 5 * rows - quarter
        if fill:
            last = jnp.concatenate([last, jnp.zeros((fill, 128), F32)], axis=0)
        out_ref[y, 5 * rows :, :] = last.astype(BF)


def first_grad_kernel(own_ref, prob_ref, peer_ref, hid_ref, out_ref, sh_ref, acc_ref):
    for k, p in enumerate((prob_ref[...], peer_ref[:, W0:])):
        p = p.astype(F32)
        for a in range(0, FW, 128):
            b = min(a + 128, FW)
            sh_ref[k * SLOTS : (k + 1) * SLOTS, a:b] = (
                p[:, : b - a] * hid_ref[k * SLOTS : (k + 1) * SLOTS, a:b]
            ).astype(BF)
    partial_grad(own_ref, peer_ref, sh_ref, out_ref, acc_ref)


def second_grad_kernel(own_ref, peer_ref, sh_ref, after_ref, out_ref, acc_ref):
    partial_grad(own_ref, peer_ref, sh_ref, out_ref, acc_ref)


def gate_kernel(x_ref, *refs):
    pass


def unpacked_sum(ref, rows):
    total = ref[0].astype(F32)
    for n in range(1, NY):
        total += ref[n].astype(F32)
    last = total[5 * rows : 5 * rows + rows // 4]
    return jnp.concatenate(
        [total[rows * j : rows * (j + 1)] for j in range(5)]
        + [jnp.concatenate([last[:, 32 * n : 32 * (n + 1)] for n in range(4)], axis=0)],
        axis=1,
    )


def sum_kernel(x0_ref, x1_ref, out_ref):
    x0, x1 = unpacked_sum(x0_ref, R0), unpacked_sum(x1_ref, R1)
    out_ref[...] = jnp.concatenate(
        [part[n * z : n * (z + 1)] for z in range(NZ) for part, n in ((x0, R0 // NZ), (x1, R1 // NZ))],
        axis=0,
    ).astype(BF)


def last_kernel(x_ref, out_ref):
    total = x_ref[0].astype(F32)
    for n in range(1, NZ):
        total += x_ref[n].astype(F32)
    out_ref[...] = total


def pre_kernel(w_ref, r0_ref, r1_ref, gate_ref, up_ref, pg_ref, sg_ref):
    lane = lax.broadcasted_iota(jnp.int32, (16, 128), 1)
    prob = lax.dot_general(
        one_hot(lane == 0), r0_ref[:, 2 * W0 :], LANES_T, preferred_element_type=F32
    )[:1]
    proj = lax.dot_general(
        w_ref[:, : 2 * W0], r0_ref[:, : 2 * W0], LANES_T, preferred_element_type=F32
    ) + lax.dot_general(w_ref[:, 2 * W0 :], r1_ref[...], LANES_T, preferred_element_type=F32)
    gate = gate_ref[...].astype(F32)
    up = up_ref[...].astype(F32)
    sig = jax.nn.sigmoid(gate)
    act = gate * sig
    part = jnp.sum(act * up * proj, axis=0, keepdims=True)
    sg_ref[...] = jnp.where(pl.program_id(0) == 0, part, part + sg_ref[...])
    hg = prob * proj
    pg_ref[0] = (hg * up * sig * (1.0 + gate * (1.0 - sig))).astype(BF)
    pg_ref[1] = (hg * act).astype(BF)


def back_kernel(here_ref, picks_ref, pos_ref, every_ref, out_ref):
    lane = lax.broadcasted_iota(jnp.int32, (SLOTS, TOK), 0)
    row = lax.broadcasted_iota(jnp.int32, (12, TOK), 0)
    for g in range(3):
        pick = picks_ref[g : g + 1, :]
        rank = pos_ref[g : g + 1, :] - 32 * pick
        at = jnp.where(lane == rank + 32 * here_ref[0], 1.0, 0.0)
        got = jnp.dot(
            every_ref[...], at, preferred_element_type=F32, precision=lax.Precision.HIGHEST
        )
        out_ref[g : g + 1, :] = jnp.sum(
            jnp.where(row == NX * g + pick, got, 0.0), axis=0, keepdims=True
        )


SMEM = pl.BlockSpec(memory_space=pltpu.SMEM)
AFTER = pl.BlockSpec(memory_space=pl.ANY)


def full(*shape):
    return pl.BlockSpec(shape, lambda i: (0,) * len(shape))


def block(rows, columns, at):
    return pl.BlockSpec((rows, columns), lambda i: (0, at))


def call(kernel, name, outs, in_specs, scratch=(), macs=0, mbytes=4, mib=63, steps=1, out_specs=None):
    shapes = tuple(jax.ShapeDtypeStruct(s, t) for s, t in outs)
    return pl.pallas_call(
        kernel,
        grid=(steps,),
        out_shape=shapes,
        in_specs=in_specs,
        out_specs=out_specs or tuple(full(*s) for s, _ in outs),
        scratch_shapes=[pltpu.VMEM(s, t) for s, t in scratch],
        compiler_params=pltpu.CompilerParams(vmem_limit_bytes=mib * 1024 * 1024),
        cost_estimate=pl.CostEstimate(
            flops=2 * macs, bytes_accessed=mbytes * 1_000_000, transcendentals=0
        ),
        name=name,
    )


def gate(x, *after):
    return pl.pallas_call(
        gate_kernel,
        out_shape=jax.ShapeDtypeStruct(x.shape, x.dtype),
        in_specs=[AFTER] * (1 + len(after)),
        out_specs=AFTER,
        input_output_aliases={0: 0},
        compiler_params=pltpu.CompilerParams(vmem_limit_bytes=63 * 1024 * 1024),
        name="gate",
    )(x, *after)


def on_device(out_grad, probs, picks, saved_pre, down_weight):
    def scalar(name):
        return lax.axis_index(name).astype(jnp.int32).reshape(1)

    core = scalar("c")
    swap = [(0, 1), (1, 0)]
    q0, q1 = split_matrix(0, FIRST), split_matrix(FIRST, OWN - FIRST)
    sp_t = saved_pre.T
    w_t = down_weight[0].T

    def exchange(blocks, axes):
        return lax.all_to_all(blocks, axes, split_axis=0, concat_axis=0, tiled=True)

    def dispatch(rows):
        return exchange(rows.reshape(12, 32, -1), ("zl", "x")).reshape(SLOTS, -1)

    send0, pos = call(
        first_pick_kernel, "first_pick",
        [((SLOTS, 2 * W0 + 128), BF), ((3, TOK), jnp.int32)],
        [SMEM, full(3, TOK), full(3, TOK), full(TOK, D), full(*q0.shape)],
        [((TOK, 2 * W0), BF)], 200_000_000,
    )(core, picks.T, probs.T, out_grad, q0)
    recv0 = dispatch(send0)
    (hid,) = call(
        hidden_kernel, "hidden", [((2 * SLOTS, FW), F32)],
        [full(2 * FW, SLOTS), full(2 * FW, SLOTS), AFTER], (), 500_000_000,
    )(sp_t, lax.ppermute(sp_t, "c", swap), pos)
    (w_ord,) = call(
        order_kernel, "order", [((FW, D), BF)],
        [SMEM, pl.BlockSpec((FW // 3, D), lambda i: (i, 0)), full(*q0.shape), full(*q1.shape), AFTER],
        (), 1_000_000_000, 10, 63, 3, (pl.BlockSpec((FW // 3, D), lambda i: (i, 0)),),
    )(core, w_t, q0, q1, hid)
    (send1,) = call(
        second_pick_kernel, "second_pick", [((SLOTS, 2 * W1), BF)],
        [SMEM, full(3, TOK), full(TOK, D), full(*q1.shape), AFTER],
        [((TOK, 2 * W1), BF)], 200_000_000,
    )(core, pos, out_grad, q1, w_ord)
    recv1 = dispatch(send1)

    recv0 = gate(recv0, send1)
    peer0 = lax.ppermute(recv0[:, W0:], "c", swap)
    part0, sh = call(
        first_grad_kernel, "first_grad",
        [((NY, 512, 128), BF), ((2 * SLOTS, FW), BF)],
        [block(SLOTS, W0, 0), block(SLOTS, 128, 2 * W0 // 128), full(SLOTS, W0 + 128),
         full(2 * SLOTS, FW)],
        [((W0, FW), F32)], 400_000_000, 6,
    )(recv0, recv0, peer0, hid)
    got0 = exchange(part0, "y")
    recv1 = gate(recv1, part0)
    peer1 = lax.ppermute(recv1[:, W1:], "c", swap)
    third = FW // 3
    pg_t, slot_grad = call(
        pre_kernel, "pre", [((2, FW, SLOTS), BF), ((1, SLOTS), F32)],
        [pl.BlockSpec((third, D), lambda i: (i, 0)), full(SLOTS, 2 * W0 + 128), full(SLOTS, 2 * W1),
         pl.BlockSpec((third, SLOTS), lambda i: (i, 0)),
         pl.BlockSpec((third, SLOTS), lambda i: (3 + i, 0))],
        (), 700_000_000, 9, 63, 3,
        (pl.BlockSpec((2, third, SLOTS), lambda i: (0, i, 0)), full(1, SLOTS)),
    )(w_ord, recv0, recv1, sp_t, sp_t)
    (part1,) = call(
        second_grad_kernel, "second_grad", [((NY, 336, 128), BF)],
        [block(SLOTS, W1, 0), full(SLOTS, W1), full(2 * SLOTS, FW), AFTER],
        [((W1, FW), F32)], 270_000_000, 4,
    )(recv1, peer1, sh, slot_grad)
    row = lax.all_gather(slot_grad, "x", axis=0, tiled=True)
    part1 = gate(part1, got0, row)
    got1 = exchange(part1, "y")
    every = lax.all_gather(gate(row, part1), "zl", axis=0, tiled=True)
    (prob_t,) = call(
        back_kernel, "back", [((3, TOK), F32)],
        [SMEM, full(3, TOK), full(3, TOK), full(12, SLOTS)], (), 1_000_000, 1,
    )(scalar("zl") * NX + scalar("x"), picks.T, pos, every)
    (sums,) = call(
        sum_kernel, "sum", [((NZ * OWN, FW), BF)],
        [full(NY, 512, 128), full(NY, 336, 128)], (), 1_000_000, 2,
    )(got0, gate(got1, prob_t))
    over_z = exchange(sums.reshape(NZ, OWN, FW), "z")
    (down_grad,) = call(
        last_kernel, "last", [((OWN, FW), F32)], [full(NZ, OWN, FW)], (), 1_000_000, 1, 16,
    )(over_z)
    return (pg_t.reshape(2 * FW, SLOTS).T, down_grad[None], prob_t.T)


def solution(mesh):
    names = ("y", "z", "c", "zl", "x")
    cut = Mesh(mesh.devices.reshape(NY, NZ, NC, NZL, NX), names)
    rows = P(names, None)
    in_specs = (rows, rows, rows, rows, P(("zl", "x"), None, None))
    out_specs = (rows, P(("zl", "x"), ("y", "z", "c"), None), rows)
    return jax.shard_map(
        on_device, mesh=cut, in_specs=in_specs, out_specs=out_specs, check_vma=False
    )
```
